256 devices in a mesh: rep: 32 (over y, z_hi, core), fsdp: 8 (over x, z_lo).
Axes of the slice: x: 4, y: 4, z: 8 (z_hi: 4, z_lo: 2; z = z_hi * 2 + z_lo), core: 2. Of those that a mesh axis runs over, the one named last changes fastest.
Arguments:
- layer_input: bfloat16 [65536, 4096], P(('rep', 'fsdp')), may hold values from -24 to 24
- norm_gain: bfloat16 [32, 4096], P('rep', 'fsdp'), may hold values from 0.25 to 1.75
- kv_weight: bfloat16 [32, 4096, 1024], P('rep', 'fsdp'), may hold values from -0.09375 to 0.09375
- kv_cotangent: bfloat16 [65536, 1024], P(('rep', 'fsdp')), may hold values from -6 to 6
- fragment_local: bfloat16 [32, 2048, 4096], P('rep', 'fsdp'), may hold values from -6 to 6
- outer_params: float32 [4, 2048, 4096], P(None, 'fsdp', 'rep'), may hold values from -6 to 6
- outer_momentum: float32 [4, 2048, 4096], P(None, 'fsdp', 'rep'), may hold values from -4 to 4
- fragment_index: int32 [1], replicated, may hold values from 0 to 3
Outputs:
- kv_out: bfloat16 [65536, 1024], P(('rep', 'fsdp'))
- input_grad: bfloat16 [65536, 4096], P(('rep', 'fsdp'))
- weight_grad: bfloat16 [32, 4096, 1024], P('rep', 'fsdp')
- gain_grad: bfloat16 [32, 4096], P('rep', 'fsdp')
- new_params: float32 [2048, 4096], P('fsdp', 'rep')
- new_momentum: float32 [2048, 4096], P('fsdp', 'rep')
- synced: bfloat16 [2048, 4096], P('fsdp')
The draws below stay inside these ranges and needn't reach their ends.
All inputs are finite; a program needn't handle non-finite values.
Results may differ from the reference program's by a relative error of at most 0.019.
Values may be sent and summed in bfloat16 or wider, within the bound.
A program may use at most 128 MiB of HBM per device.

```python
import jax
import jax.numpy as jnp
from jax import lax

D = 4096
FRAGS = 4
TOK_DEV = 256
KV = 1024
FRAG_ROWS = 2048
REPS = 32
TOK_REP = 2048
TOKENS = 65536
N_FSDP = 8


def with_spikes(values, stream_key, source, target, shards_of, factor):
    owner, partner = [(jnp.arange(values.shape[position]) // (values.shape[position] // shards_of)).reshape([-1 if axis == position else 1 for axis in range(values.ndim)]) for position in (source, target)]
    chosen = jax.random.permutation(stream_key, shards_of)[partner]
    strong = (owner == chosen) | (owner == (partner + shards_of // 2) % shards_of)
    return jnp.where(strong, factor * values, values)


def levels(own_key, dims, split, low, top_value):
    level, own = 1.0, jax.random.fold_in(own_key, 6)
    for dim, parts in split:
        steps = jnp.exp(jax.random.uniform(jax.random.fold_in(own, dim), (parts,), jnp.float32, low / len(split), top_value / len(split)))
        level = level * jnp.repeat(steps, dims[dim] // parts).reshape([-1 if axis == dim else 1 for axis in range(len(dims))])
    return level


def scatter_about(stream_key, dims, deviation, reach, pieces=(), kind=jnp.bfloat16):
    drawn = deviation * jax.random.normal(stream_key, dims, jnp.float32)
    if pieces:
        drawn = drawn * levels(stream_key, dims, pieces, -0.22, 0.18)
    return jnp.clip(drawn, -reach, reach).astype(kind)


def heavy_noise(own_key, dims, scale, reach, pieces, heavy, kind=jnp.bfloat16):
    drawn = scale * jax.random.normal(own_key, dims, jnp.float32)
    if pieces:
        drawn = drawn * levels(own_key, dims, pieces, -0.22, 0.18)
    return jnp.clip(with_spikes(drawn, jax.random.fold_in(own_key, 3), *heavy), -reach, reach).astype(kind)


def setup_inputs(seed: int = 0) -> dict:
    arg_keys = jax.random.split(jax.random.key(seed), 9)
    return {
        "layer_input": heavy_noise(arg_keys[0], (TOKENS, D), 1.0, 24.0, ((0, 256),), (0, 1, 256, 6.0)),
        "norm_gain": jnp.clip(1.0 + 0.15 * jax.random.normal(arg_keys[1], (REPS, D), jnp.float32), 0.25, 1.75).astype(jnp.bfloat16),
        "kv_weight": scatter_about(arg_keys[2], (REPS, D, KV), D ** -0.5, 0.09375, ((0, 32), (1, 8))),
        "kv_cotangent": scatter_about(arg_keys[3], (TOKENS, KV), 1.0, 6.0, ((0, 256),)),
        "fragment_local": heavy_noise(arg_keys[4], (REPS, FRAG_ROWS, D), 1.0, 6.0, ((0, 32), (1, 8)), (0, 2, 32, 2.75)),
        "outer_params": scatter_about(arg_keys[5], (FRAGS, FRAG_ROWS, D), 1.0, 6.0, ((1, 8), (2, 32)), jnp.float32),
        "outer_momentum": scatter_about(arg_keys[6], (FRAGS, FRAG_ROWS, D), 0.5, 4.0, ((1, 8), (2, 32)), jnp.float32),
        "fragment_index": jax.random.randint(arg_keys[7], (1,), 0, FRAGS).astype(jnp.int32),
    }


def layer_one(inputs):
    rows, gain, weight, cotangent = inputs
    wide_rows = rows.astype(jnp.float32)
    inverse = lax.rsqrt(lax.optimization_barrier(jnp.mean(wide_rows * wide_rows, axis=-1, keepdims=True)) + 1e-05)
    unit_rows = wide_rows * inverse
    gain_wide = gain.astype(jnp.float32)
    normed = (unit_rows * gain_wide).astype(jnp.bfloat16)
    kv_out = jnp.dot(normed, weight, preferred_element_type=jnp.float32).astype(jnp.bfloat16)
    hidden = jnp.dot(cotangent, weight.T, preferred_element_type=jnp.float32)
    block_normed = normed.astype(jnp.float32).reshape(N_FSDP, TOK_DEV, D)
    block_cotangent = cotangent.astype(jnp.float32).reshape(N_FSDP, TOK_DEV, KV)
    weight_parts = jnp.einsum('btd,btk->bdk', block_normed, block_cotangent).astype(jnp.bfloat16)
    weight_grad = lax.optimization_barrier(jnp.sum(weight_parts.astype(jnp.float32), axis=0)).astype(jnp.bfloat16)
    gain_parts = lax.optimization_barrier(jnp.sum((hidden * unit_rows).reshape(N_FSDP, TOK_DEV, D), axis=1)).astype(jnp.bfloat16)
    gain_grad = lax.optimization_barrier(jnp.sum(gain_parts.astype(jnp.float32), axis=0)).astype(jnp.bfloat16)
    scaled = hidden * gain_wide
    inner_mean = lax.optimization_barrier(jnp.mean(scaled * unit_rows, axis=-1, keepdims=True))
    input_grad = (inverse * (scaled - unit_rows * inner_mean)).astype(jnp.bfloat16)
    return (kv_out, input_grad, weight_grad, gain_grad)

def reference(layer_input, norm_gain, kv_weight, kv_cotangent, fragment_local, outer_params, outer_momentum, fragment_index):
    rows = layer_input.reshape(REPS, TOK_REP, D)
    cotangent = kv_cotangent.reshape(REPS, TOK_REP, KV)
    kv_out, input_grad, weight_grad, gain_grad = lax.map(layer_one, (rows, norm_gain, kv_weight, cotangent))
    kv_out = kv_out.reshape(TOKENS, KV)
    input_grad = input_grad.reshape(TOKENS, D)

    def add_replica(running, replica_rows):
        return (running + replica_rows.astype(jnp.float32), None)
    summed, unused = lax.scan(add_replica, jnp.zeros((FRAG_ROWS, D), jnp.float32), fragment_local)
    average = summed / REPS
    chosen = fragment_index[0].astype(jnp.int32)
    params_now = lax.dynamic_index_in_dim(outer_params, chosen, 0, keepdims=False)
    moment_now = lax.dynamic_index_in_dim(outer_momentum, chosen, 0, keepdims=False)
    pseudo_grad = params_now - average
    new_momentum = 0.9 * moment_now + pseudo_grad
    new_params = params_now - 0.7 * (pseudo_grad + 0.9 * new_momentum)
    synced = new_params.astype(jnp.bfloat16)
    return (kv_out, input_grad, weight_grad, gain_grad, new_params, new_momentum, synced)
```

```python
import jax
import jax.numpy as jnp
from jax import lax
from jax.experimental import pallas as pl
from jax.experimental.pallas import tpu as pltpu
from jax.sharding import PartitionSpec as P

MESH = pl.DeviceIdType.MESH
F32, BF16 = jnp.float32, jnp.bfloat16
D = 4096
ROWS = 256
BLK = 512
KV = 1024
CH = 32

N_COT, N_X, N_W, N_WF, N_GAIN, N_INV = 0, 1, 5, 7, 9, 12
N_S2, N_S1P, N_S1S, N_INNER, N_KV, N_DX, N_GG = 13, 15, 17, 19, 20, 21, 25
N_FR, N_Y1, N_Y2, N_Z, N_ZG, N_G1, N_G2, N_SY = 28, 32, 34, 36, 39, 42, 44, 46
N_REMOTE = 50
L_X, L_C, L_W, L_FR, L_OP, L_OM, L_DX, L_DW, L_KV, L_NP, L_NM, L_SY = (
    0, 8, 9, 10, 14, 15, 16, 20, 21, 22, 23, 24,
)
N_LOCAL = 28


def wide(value, times):
    return jnp.concatenate([value] * times, axis=1)


def kernel(
    x_hbm, gain_ref, w_hbm, c_hbm, fr_hbm, op_hbm, om_hbm, idx_ref,
    kv_out, dx_out, dw_out, dg_out, np_out, nm_out, sy_out,
    xv, xp, cv, wv, gv, inv, nv, hv, kacc, d0, d13, s2, s2r, s1, s1r,
    inn, ins, inr, kvs, kvr, kvo, dxs, dxo, dwo, gs, gr,
    fo, fr, f2, y1r, f13, y2r, gb, g0, zr, opv, omv, npv, nmv, sy, sp, asm,
    ssem, rsem, lsem,
):
    f, r = lax.axis_index("fsdp"), lax.axis_index("rep")
    x, z = f // 2, f % 2
    y, zh, c = r // 8, (r // 2) % 4, r % 2

    def at_x(step):
        return {"fsdp": ((x + step) % 4) * 2 + z}

    def at_y(step):
        return {"rep": ((y + step) % 4) * 8 + zh * 2 + c}

    def at_zh(step):
        return {"rep": y * 8 + ((zh + step) % 4) * 2 + c}

    pair, core = {"fsdp": x * 2 + 1 - z}, {"rep": y * 8 + zh * 2 + 1 - c}

    def remote(number, source, target, device):
        return pltpu.make_async_remote_copy(
            src_ref=source, dst_ref=target, send_sem=ssem.at[number], recv_sem=rsem.at[number],
            device_id=device, device_id_type=MESH,
        )

    def local(number, source, target):
        return pltpu.make_async_copy(source, target, lsem.at[number])

    def own_cols(j):
        return pl.ds(pl.multiple_of((((x + j) % 4) * 2 + z) * BLK, BLK), BLK)

    def pair_cols(j):
        return pl.ds(pl.multiple_of((((x + j) % 4) * 2 + 1 - z) * BLK, BLK), BLK)

    def y_cols(k):
        return pl.ds(pl.multiple_of(((y + k) % 4) * 1024, 1024), 1024)

    low, high = pl.ds(0, ROWS), pl.ds(ROWS, ROWS)

    cot = remote(N_COT, c_hbm, cv.at[high], pair)
    rows = [remote(N_X + j, x_hbm.at[:, pair_cols(j)], xp.at[j], pair) for j in range(4)]
    w_right = remote(N_W, w_hbm.at[0], wv.at[3], at_x(1))
    w_left = remote(N_W + 1, w_hbm.at[0], wv.at[1], at_x(3))
    wf_right = remote(N_WF, wv.at[3, low], wv.at[2, low], at_x(1))
    wf_left = remote(N_WF + 1, wv.at[1, high], wv.at[2, high], at_x(3))
    gains = [remote(N_GAIN + m - 1, gv.at[0], gv.at[4 - m], at_x(m)) for m in (1, 2, 3)]
    inverse = remote(N_INV, inn.at[0], inn.at[1], pair)
    s2_right = remote(N_S2, s2.at[0], s2r.at[0], at_x(1))
    s2_left = remote(N_S2 + 1, s2.at[1], s2r.at[1], at_x(3))
    s1p_right = remote(N_S1P, s1.at[0, high], s1r.at[0, high], at_x(1))
    s1p_left = remote(N_S1P + 1, s1.at[1, low], s1r.at[1, low], at_x(3))
    s1s_right = remote(N_S1S, s1.at[0, low], s1r.at[0, low], at_x(1))
    s1s_left = remote(N_S1S + 1, s1.at[1, high], s1r.at[1, high], at_x(3))
    inner = remote(N_INNER, ins, inr, pair)
    kv_half = remote(N_KV, kvs, kvr, pair)
    dx_half = [remote(N_DX + j, dxs.at[j], dx_out.at[:, own_cols(j)], pair) for j in range(4)]
    gain_sum = [remote(N_GG + m - 1, gs.at[m], gr.at[m], at_x(m)) for m in (1, 2, 3)]
    frag = [remote(N_FR + k, fr_hbm.at[0, :, y_cols(k)], fr.at[k], core) for k in range(4)]
    y1_right = remote(N_Y1, f2.at[pl.ds(0, 128)], y1r.at[0], at_y(1))
    y1_left = remote(N_Y1 + 1, f2.at[pl.ds(128, 128)], y1r.at[1], at_y(3))
    y2_right = remote(N_Y2, f13.at[0], y2r.at[0], at_y(1))
    y2_left = remote(N_Y2 + 1, f13.at[1], y2r.at[1], at_y(3))
    z_sum = [remote(N_Z + m - 1, gb.at[m], zr.at[m], at_zh(m)) for m in (1, 2, 3)]
    sy_cols = pl.ds(pl.multiple_of(zh * 128, 128), 128)
    z_gather = [
        remote(N_ZG + m - 1, sy.at[0, :, sy_cols], sy.at[0, :, sy_cols], at_zh(m))
        for m in (1, 2, 3)
    ]
    g1_right = remote(N_G1, sy.at[0], sy.at[3], at_y(1))
    g1_left = remote(N_G1 + 1, sy.at[0], sy.at[1], at_y(3))
    top, bottom = pl.ds(0, 128), pl.ds(128, 128)
    g2_right = remote(N_G2, sy.at[3, top], sy.at[2, top], at_y(1))
    g2_left = remote(N_G2 + 1, sy.at[1, bottom], sy.at[2, bottom], at_y(3))
    to_core = [remote(N_SY + k, sy.at[k], sp.at[k], core) for k in range(4)]

    load_x = [local(L_X + j, x_hbm.at[:, own_cols(j)], xv.at[j]) for j in range(4)]
    load_x += [local(L_X + 4 + j, x_hbm.at[:, pair_cols(j)], xv.at[4 + j]) for j in range(4)]
    load_c = local(L_C, c_hbm, cv.at[low])
    load_w = local(L_W, w_hbm.at[0], wv.at[0])
    load_fr = [local(L_FR + k, fr_hbm.at[0, :, y_cols(k)], fo.at[k]) for k in range(4)]
    load_op, load_om = local(L_OP, op_hbm, opv), local(L_OM, om_hbm, omv)
    for copy in load_x + [load_c, load_w] + load_fr + [load_op, load_om]:
        copy.start()

    barrier = pltpu.get_barrier_semaphore()
    partners = [pair, core] + [at_x(m) for m in (1, 2, 3)]
    partners += [at_y(1), at_y(3)] + [at_zh(m) for m in (1, 2, 3)]
    for device in partners:
        pl.semaphore_signal(barrier, inc=1, device_id=device, device_id_type=MESH)
    gv[0] = jnp.broadcast_to(gain_ref[...].astype(F32), (8, BLK))
    pl.semaphore_wait(barrier, len(partners))

    for copy in gains:
        copy.start()
    w_right.start()
    w_left.start()
    cot.start()
    for j in (2, 1, 3, 0):
        rows[j].start()
    for k in (2, 1, 3, 0):
        frag[k].start()

    def chunks(count, body, carry=0, size=CH):
        def step(i, held):
            return body(pl.ds(pl.multiple_of(i * size, size), size), held)
        return lax.fori_loop(0, count // size, step, carry)

    def statistics(at, held):
        total = jnp.zeros((CH, BLK), F32)
        for j in range(8):
            value = xv[j, at, :].astype(F32)
            total = total + value * value
        mean = jnp.sum(total, axis=1, keepdims=True) * (1.0 / D)
        inv[0, at, :] = jnp.broadcast_to(lax.rsqrt(mean + 1e-05), (CH, 128))
        return held

    def normalise(j, half):
        source = xv if half == 0 else xp

        def step(at, held):
            unit = source[j, at, :].astype(F32) * wide(inv[half, at, :], BLK // 128)
            rows_at = pl.ds(pl.multiple_of(at.start + half * ROWS, CH), CH)
            nv[j, rows_at, :] = (unit * gv[j, 0:1, :]).astype(BF16)
            return held

        chunks(ROWS, step)

    def add_kv(j, first):
        def step(t, held):
            cols = pl.ds(pl.multiple_of(t * 256, 256), 256)
            part = jnp.dot(nv[j], wv[j, :, cols], preferred_element_type=F32)
            if first:
                kacc[:, cols] = part
            else:
                kacc[:, cols] += part
            return held

        lax.fori_loop(0, KV // 256, step, 0)

    def make_hidden(j):
        def step(t, held):
            at = pl.ds(pl.multiple_of(t * 256, 256), 256)
            hv[j, :, at] = lax.dot_general(
                cv[...], wv[j, at, :], (((1,), (1,)), ((), ())), preferred_element_type=F32
            )
            return held

        lax.fori_loop(0, BLK // 256, step, 0)

    def weight_term(j, half, put):
        def step(t, held):
            cols = pl.ds(pl.multiple_of(t * 512, 512), 512)
            put(cols, lax.dot_general(
                nv[j, :, pl.ds(half * 256, 256)], cv[:, cols], (((0,), (0,)), ((), ())),
                preferred_element_type=F32,
            ))
            return held

        lax.fori_loop(0, KV // 512, step, 0)

    def into(ref, *where):
        def put(cols, value):
            ref[(*where, cols)] = value.astype(ref.dtype)
        return put

    for copy in load_x:
        copy.wait()
    chunks(ROWS, statistics)
    for half in range(2):
        part = pl.ds(half * 128, 128)
        inn[0, :, part] = jnp.transpose(inv[0, part, :])[0:8, :]
    inverse.start()
    for copy in gains:
        copy.wait_recv()
    for j in (2, 1, 3, 0):
        normalise(j, 0)

    def own_part(k, zz):
        return pl.ds(pl.multiple_of(zz * 256 + c * 128, 128), 128)

    def pair_sum(k, at, zz):
        cols = own_part(k, zz)
        return fo[k, at, cols].astype(F32) + fr[k, at, cols].astype(F32)

    for k in range(4):
        load_fr[k].wait()
    frag[2].wait_recv()

    def sum_f2(at, held):
        for zz in range(4):
            f2[at, pl.ds(zz * 128, 128)] = pair_sum(2, at, zz).astype(BF16)
        return held

    chunks(256, sum_f2)
    y1_right.start()
    y1_left.start()

    load_c.wait()
    load_w.wait()
    cot.wait_recv()
    make_hidden(0)

    inverse.wait_recv()
    for half in range(2):
        part = pl.ds(half * 128, 128)
        inv[1, part, :] = jnp.transpose(jnp.broadcast_to(inn[1, 0:1, part], (128, 128)))
    rows[2].wait_recv()
    normalise(2, 1)
    weight_term(2, 0, into(s2, 0, slice(None)))
    s2_right.start()
    weight_term(2, 1, into(s2, 1, slice(None)))
    s2_left.start()

    y1_right.wait_recv()
    y1_left.wait_recv()
    for side, k, half in ((0, 1, 0), (1, 3, 1)):
        frag[k].wait_recv()

        def sum_f13(at, held, side=side, k=k):
            for zz in range(4):
                f13[side, at, pl.ds(zz * 128, 128)] = pair_sum(k, at, zz).astype(BF16)
            return held

        def sum_f13_with(at, held, side=side, k=k, half=half):
            there = pl.ds(pl.multiple_of(at.start + half * 128, CH), CH)
            for zz in range(4):
                cols = pl.ds(zz * 128, 128)
                total = pair_sum(k, there, zz) + y1r[side, at, cols].astype(F32)
                f13[side, there, cols] = total.astype(BF16)
            return held

        def sum_f13_plain(at, held, side=side, k=k, half=half):
            there = pl.ds(pl.multiple_of(at.start + (1 - half) * 128, CH), CH)
            return sum_f13(there, held, side, k)

        chunks(128, sum_f13_with)
        chunks(128, sum_f13_plain)
    y2_right.start()
    y2_left.start()

    rows[1].wait_recv()
    normalise(1, 1)
    weight_term(1, 1, into(s1, 0, high))
    s1p_right.start()
    weight_term(1, 0, into(d13, 0, slice(None)))
    rows[3].wait_recv()
    normalise(3, 1)
    weight_term(3, 0, into(s1, 1, low))
    s1p_left.start()
    weight_term(3, 1, into(d13, 1, slice(None)))

    w_right.wait_recv()
    wf_right.start()
    w_left.wait_recv()
    wf_left.start()

    frag[0].wait_recv()
    y2_right.wait_recv()
    y2_left.wait_recv()

    def sum_g(m):
        zz = (zh + m) % 4
        cols = pl.ds(pl.multiple_of(zz * 128, 128), 128)

        def step(at, held):
            total = pair_sum(0, at, zz)
            total = total + y2r[0, at, cols].astype(F32) + y2r[1, at, cols].astype(F32)
            if m == 0:
                g0[at, :] = total
            else:
                gb[m, at, :] = total.astype(BF16)
            return held

        chunks(256, step)

    for m in (2, 1, 3):
        sum_g(m)
        z_sum[m - 1].start()
    sum_g(0)

    add_kv_first = True
    make_hidden(1)
    make_hidden(3)
    rows[0].wait_recv()
    normalise(0, 1)
    for j in (0, 1, 3):
        add_kv(j, add_kv_first)
        add_kv_first = False

    s2_right.wait_recv()

    def add_passing(side, first_row):
        def step(at, held):
            there = pl.ds(pl.multiple_of(at.start + first_row, CH), CH)
            s1[side, there, :] = (d13[side, at, :] + s2r[side, at, :].astype(F32)).astype(BF16)
            return held
        chunks(256, step)

    add_passing(0, 0)
    s1s_right.start()
    s2_left.wait_recv()
    add_passing(1, 256)
    s1s_left.start()

    for copy in z_sum:
        copy.wait_recv()
    load_op.wait()
    load_om.wait()
    chosen = idx_ref[0]

    def update(at, held):
        total = g0[at, :]
        for m in (1, 2, 3):
            total = total + zr[m, at, :].astype(F32)
        now = opv[chosen, at, :]
        pseudo = now - total * (1.0 / 32.0)
        moment = 0.9 * omv[chosen, at, :] + pseudo
        new = now - 0.7 * (pseudo + 0.9 * moment)
        nmv[at, :] = moment
        npv[at, :] = new
        sy[0, at, sy_cols] = new.astype(BF16)
        return held

    chunks(256, update)
    for copy in z_gather:
        copy.start()
    store_np, store_nm = local(L_NP, npv, np_out), local(L_NM, nmv, nm_out)
    store_np.start()
    store_nm.start()

    weight_term(0, 0, into(d0, low))
    weight_term(0, 1, into(d0, high))

    for copy in z_gather:
        copy.wait_recv()
    g1_right.start()
    g1_left.start()
    to_core[0].start()

    wf_right.wait_recv()
    wf_left.wait_recv()
    add_kv(2, False)

    def inner_term(at, held):
        product = jnp.zeros((CH, 256), F32)
        for t in range(4):
            cols = pl.ds(t * 256, 256)
            product = product + cv[at, cols].astype(F32) * kacc[at, cols]
        total = jnp.sum(product, axis=1, keepdims=True) * (1.0 / D)
        inv[2, at, :] = jnp.broadcast_to(total, (CH, 128))
        return held

    def inner_all(at, held):
        product = jnp.zeros((CH, 256), F32)
        for t in range(4):
            cols = pl.ds(t * 256, 256)
            product = product + cv[at, cols].astype(F32) * kacc[at, cols]
        total = jnp.sum(product, axis=1, keepdims=True) * (1.0 / D)
        return total

    def inner_step(half):
        def step(at, held):
            there = pl.ds(pl.multiple_of(at.start + half * ROWS, CH), CH)
            inv[2 + half, at, :] = jnp.broadcast_to(inner_all(there, held), (CH, 128))
            return held
        chunks(ROWS, step)

    for half in range(2):
        inner_step(half)
        for part in range(2):
            there = pl.ds(half * ROWS + part * 128, 128)
            ins[:, there] = jnp.transpose(inv[2 + half, pl.ds(part * 128, 128), :])[0:8, :]
    inner.start()

    def round_kv(at, held):
        there = pl.ds(pl.multiple_of(at.start + ROWS, CH), CH)
        kvs[at, :] = kacc[there, :].astype(BF16)
        return held

    chunks(ROWS, round_kv)
    kv_half.start()
    make_hidden(2)

    g1_right.wait_recv()
    g2_right.start()
    g1_left.wait_recv()
    g2_left.start()
    to_core[3].start()
    to_core[1].start()

    inner.wait_recv()
    for half in range(2):
        for part in range(2):
            mine = pl.ds(half * ROWS + part * 128, 128)
            theirs = pl.ds((1 - half) * ROWS + part * 128, 128)
            total = ins[0:1, mine] + inr[0:1, theirs]
            inv[2 + half, pl.ds(part * 128, 128), :] = jnp.transpose(
                jnp.broadcast_to(total, (128, 128))
            )

    def input_grad(j, half, target):
        source = xv if half == 0 else xp

        def step(at, held):
            there = pl.ds(pl.multiple_of(at.start + half * ROWS, CH), CH)
            scale = wide(inv[half, at, :], BLK // 128)
            unit = source[j, at, :].astype(F32) * scale
            hidden = hv[j, there, :]
            term = (hidden * unit).reshape(CH // 8, 8, BLK)
            scaled = hidden * gv[j, 0:1, :]
            mean = wide(inv[2 + half, at, :], BLK // 128)
            target[j, at, :] = (scale * (scaled - unit * mean)).astype(BF16)
            return held + jnp.sum(term, axis=0)

        return chunks(ROWS, step, jnp.zeros((8, BLK), F32))

    for j in range(4):
        gs[j] = input_grad(j, 1, dxs)
        dx_half[j].start()
    store_dx = [local(L_DX + j, dxo.at[j], dx_out.at[:, own_cols(j)]) for j in range(4)]
    for j in (1, 2, 3, 0):
        total = gs[j] + input_grad(j, 0, dxo)
        store_dx[j].start()
        gs[j] = jnp.broadcast_to(jnp.sum(total, axis=0, keepdims=True), (8, BLK))
        if j > 0:
            gain_sum[j - 1].start()

    g2_right.wait_recv()
    g2_left.wait_recv()
    to_core[2].start()
    store_sy = [local(L_SY + k, asm.at[k], sy_out.at[:, y_cols(k)]) for k in range(4)]
    for k in (0, 3, 1, 2):
        to_core[k].wait_recv()

        def place(at, held, k=k):
            for zz in range(4):
                cols = pl.ds(zz * 128, 128)
                mine = pl.ds(pl.multiple_of(zz * 256 + c * 128, 128), 128)
                theirs = pl.ds(pl.multiple_of(zz * 256 + (1 - c) * 128, 128), 128)
                asm[k, at, mine] = sy[k, at, cols]
                asm[k, at, theirs] = sp[k, at, cols]
            return held

        chunks(256, place)
        store_sy[k].start()

    kv_half.wait_recv()

    def finish_kv(at, held):
        kvo[at, :] = (kacc[at, :] + kvr[at, :].astype(F32)).astype(BF16)
        return held

    chunks(ROWS, finish_kv)
    store_kv = local(L_KV, kvo, kv_out)
    store_kv.start()
    for copy in (s1p_right, s1p_left, s1s_right, s1s_left):
        copy.wait_recv()

    def finish_dw(at, held):
        total = d0[at, :] + s1r[0, at, :].astype(F32) + s1r[1, at, :].astype(F32)
        dwo[at, :] = total.astype(BF16)
        return held

    chunks(BLK, finish_dw)
    store_dw = local(L_DW, dwo, dw_out.at[0])
    store_dw.start()
    for copy in gain_sum:
        copy.wait_recv()
    total = gs[0, 0:1, :] + gr[1, 0:1, :] + gr[2, 0:1, :] + gr[3, 0:1, :]
    dg_out[...] = total.astype(BF16)
    for copy in dx_half:
        copy.wait_recv()

    for copy in (
        [cot, w_right, w_left, wf_right, wf_left, inverse, s2_right, s2_left]
        + [s1p_right, s1p_left, s1s_right, s1s_left, inner, kv_half]
        + [y1_right, y1_left, y2_right, y2_left, g1_right, g1_left, g2_right, g2_left]
        + rows + gains + dx_half + gain_sum + frag + z_sum + z_gather + to_core
    ):
        copy.wait_send()
    for copy in store_dx + store_sy + [store_kv, store_dw, store_np, store_nm]:
        copy.wait()


def on_device(x, gain, w, cot, frag, params, moment, index):
    any_spec = pl.BlockSpec(memory_space=pl.ANY)
    vmem = pl.BlockSpec(memory_space=pltpu.VMEM)
    out = jax.ShapeDtypeStruct
    return pl.pallas_call(
        kernel,
        out_shape=(
            out((ROWS, KV), BF16), out((ROWS, D), BF16), out((1, BLK, KV), BF16),
            out((1, BLK), BF16), out((256, 128), F32), out((256, 128), F32),
            out((256, D), BF16),
        ),
        in_specs=[any_spec, vmem] + [any_spec] * 5 + [pl.BlockSpec(memory_space=pltpu.SMEM)],
        out_specs=(any_spec, any_spec, any_spec, vmem, any_spec, any_spec, any_spec),
        scratch_shapes=[
            pltpu.VMEM((8, ROWS, BLK), BF16),
            pltpu.VMEM((4, ROWS, BLK), BF16),
            pltpu.VMEM((2 * ROWS, KV), BF16),
            pltpu.VMEM((4, BLK, KV), BF16),
            pltpu.VMEM((4, 8, BLK), F32),
            pltpu.VMEM((4, ROWS, 128), F32),
            pltpu.VMEM((4, 2 * ROWS, BLK), BF16),
            pltpu.VMEM((4, 2 * ROWS, BLK), F32),
            pltpu.VMEM((2 * ROWS, KV), F32),
            pltpu.VMEM((BLK, KV), F32),
            pltpu.VMEM((2, 256, KV), F32),
            pltpu.VMEM((2, 256, KV), BF16),
            pltpu.VMEM((2, 256, KV), BF16),
            pltpu.VMEM((2, BLK, KV), BF16),
            pltpu.VMEM((2, BLK, KV), BF16),
            pltpu.VMEM((2, 8, ROWS), F32),
            pltpu.VMEM((8, 2 * ROWS), F32),
            pltpu.VMEM((8, 2 * ROWS), F32),
            pltpu.VMEM((ROWS, KV), BF16),
            pltpu.VMEM((ROWS, KV), BF16),
            pltpu.VMEM((ROWS, KV), BF16),
            pltpu.VMEM((4, ROWS, BLK), BF16),
            pltpu.VMEM((4, ROWS, BLK), BF16),
            pltpu.VMEM((BLK, KV), BF16),
            pltpu.VMEM((4, 8, BLK), F32),
            pltpu.VMEM((4, 8, BLK), F32),
            pltpu.VMEM((4, 256, 1024), BF16),
            pltpu.VMEM((4, 256, 1024), BF16),
            pltpu.VMEM((256, 512), BF16),
            pltpu.VMEM((2, 128, 512), BF16),
            pltpu.VMEM((2, 256, 512), BF16),
            pltpu.VMEM((2, 256, 512), BF16),
            pltpu.VMEM((4, 256, 128), BF16),
            pltpu.VMEM((256, 128), F32),
            pltpu.VMEM((4, 256, 128), BF16),
            pltpu.VMEM((4, 256, 128), F32),
            pltpu.VMEM((4, 256, 128), F32),
            pltpu.VMEM((256, 128), F32),
            pltpu.VMEM((256, 128), F32),
            pltpu.VMEM((4, 256, 512), BF16),
            pltpu.VMEM((4, 256, 512), BF16),
            pltpu.VMEM((4, 256, 1024), BF16),
            pltpu.SemaphoreType.DMA((N_REMOTE,)),
            pltpu.SemaphoreType.DMA((N_REMOTE,)),
            pltpu.SemaphoreType.DMA((N_LOCAL,)),
        ],
        compiler_params=pltpu.CompilerParams(
            collective_id=0, has_side_effects=True, vmem_limit_bytes=56 * 1024 * 1024
        ),
        cost_estimate=pl.CostEstimate(
            flops=6 * ROWS * D * KV, bytes_accessed=24 << 20, transcendentals=ROWS
        ),
    )(x, gain, w, cot, frag, params, moment, index)


def solution(mesh):
    return jax.shard_map(
        on_device,
        mesh=mesh,
        in_specs=(
            P(("rep", "fsdp"), None),
            P("rep", "fsdp"),
            P("rep", "fsdp", None),
            P(("rep", "fsdp"), None),
            P("rep", "fsdp", None),
            P(None, "fsdp", "rep"),
            P(None, "fsdp", "rep"),
            P(),
        ),
        out_specs=(
            P(("rep", "fsdp"), None),
            P(("rep", "fsdp"), None),
            P("rep", "fsdp", None),
            P("rep", "fsdp"),
            P("fsdp", "rep"),
            P("fsdp", "rep"),
            P("fsdp", None),
        ),
        check_vma=False,
    )
```

```python
import jax
import jax.numpy as jnp
from jax import lax
from jax.experimental import pallas as pl
from jax.experimental.pallas import tpu as pltpu
from jax.sharding import PartitionSpec as P

MESH = pl.DeviceIdType.MESH
F32, BF16 = jnp.float32, jnp.bfloat16
D = 4096
ROWS = 256
BLK = 512
KV = 1024
CH = 32

N_COT, N_X, N_W, N_GAIN, N_INV = 0, 1, 5, 9, 12
N_WF = 50
N_S2, N_S1P, N_S1S, N_INNER, N_KV, N_DX, N_GG = 13, 15, 17, 19, 20, 21, 25
N_FR, N_Y1, N_Y2, N_Z, N_ZG, N_G1, N_G2, N_SY = 28, 32, 34, 36, 39, 42, 44, 46
N_REMOTE = 52
L_X, L_C, L_W, L_FR, L_OP, L_OM = 0, 8, 9, 10, 14, 15
N_LOCAL = 16


def wide(value, times):
    return jnp.concatenate([value] * times, axis=1)


def kernel(
    x_hbm, gain_ref, w_hbm, c_hbm, fr_hbm, op_hbm, om_hbm, idx_ref,
    kv_out, dx_out, dw_out, dg_out, np_out, nm_out, sy_out,
    xv, xp, cv, wv, gv, inv, nv, hv, kacc, d0, d13, s2, s2r, s1, s1r,
    inn, ins, inr, kvs, kvr, dxs, gs, gr,
    fo, fr, f2, y1r, f13, y2r, gb, g0, zr, opv, omv, sy, sp,
    ssem, rsem, lsem,
):
    f, r = lax.axis_index("fsdp"), lax.axis_index("rep")
    x, z = f // 2, f % 2
    y, zh, c = r // 8, (r // 2) % 4, r % 2

    def at_x(step):
        return {"fsdp": ((x + step) % 4) * 2 + z}

    def at_y(step):
        return {"rep": ((y + step) % 4) * 8 + zh * 2 + c}

    def at_zh(step):
        return {"rep": y * 8 + ((zh + step) % 4) * 2 + c}

    pair, core = {"fsdp": x * 2 + 1 - z}, {"rep": y * 8 + zh * 2 + 1 - c}

    def remote(number, source, target, device):
        return pltpu.make_async_remote_copy(
            src_ref=source, dst_ref=target, send_sem=ssem.at[number], recv_sem=rsem.at[number],
            device_id=device, device_id_type=MESH,
        )

    def local(number, source, target):
        return pltpu.make_async_copy(source, target, lsem.at[number])

    def own_cols(j):
        return pl.ds(pl.multiple_of((((x + j) % 4) * 2 + z) * BLK, BLK), BLK)

    def pair_cols(j):
        return pl.ds(pl.multiple_of((((x + j) % 4) * 2 + 1 - z) * BLK, BLK), BLK)

    def y_cols(k):
        return pl.ds(pl.multiple_of(((y + k) % 4) * 1024, 1024), 1024)

    low, high = pl.ds(0, ROWS), pl.ds(ROWS, ROWS)

    cot = remote(N_COT, c_hbm, cv.at[high], pair)
    rows = [remote(N_X + j, x_hbm.at[:, pair_cols(j)], xp.at[j], pair) for j in range(4)]
    parts = (low, high)
    w_right = [remote(N_W + h, w_hbm.at[0, parts[h]], wv.at[3, parts[h]], at_x(1)) for h in range(2)]
    w_left = [remote(N_W + 2 + h, w_hbm.at[0, parts[h]], wv.at[1, parts[h]], at_x(3)) for h in range(2)]
    wf_right = remote(N_WF, wv.at[3, low], wv.at[2, low], at_x(1))
    wf_left = remote(N_WF + 1, wv.at[1, high], wv.at[2, high], at_x(3))
    gains = [remote(N_GAIN + m - 1, gv.at[0], gv.at[4 - m], at_x(m)) for m in (1, 2, 3)]
    inverse = remote(N_INV, inn.at[0], inn.at[1], pair)
    s2_right = remote(N_S2, s2.at[0], s2r.at[0], at_x(1))
    s2_left = remote(N_S2 + 1, s2.at[1], s2r.at[1], at_x(3))
    s1p_right = remote(N_S1P, s1.at[0, high], s1r.at[0, high], at_x(1))
    s1p_left = remote(N_S1P + 1, s1.at[1, low], s1r.at[1, low], at_x(3))
    s1s_right = remote(N_S1S, s1.at[0, low], s1r.at[0, low], at_x(1))
    s1s_left = remote(N_S1S + 1, s1.at[1, high], s1r.at[1, high], at_x(3))
    inner = remote(N_INNER, ins, inr, pair)
    kv_half = remote(N_KV, kvs, kvr, pair)
    dx_half = [remote(N_DX + j, dxs.at[j], dx_out.at[:, own_cols(j)], pair) for j in range(4)]
    gain_sum = [remote(N_GG + m - 1, gs.at[m], gr.at[m], at_x(m)) for m in (1, 2, 3)]
    frag = [remote(N_FR + k, fr_hbm.at[0, :, y_cols(k)], fr.at[k], core) for k in range(4)]
    y1_right = remote(N_Y1, f2.at[pl.ds(0, 128)], y1r.at[0], at_y(1))
    y1_left = remote(N_Y1 + 1, f2.at[pl.ds(128, 128)], y1r.at[1], at_y(3))
    y2_right = remote(N_Y2, f13.at[0], y2r.at[0], at_y(1))
    y2_left = remote(N_Y2 + 1, f13.at[1], y2r.at[1], at_y(3))
    z_sum = [remote(N_Z + m - 1, gb.at[m], zr.at[m], at_zh(m)) for m in (1, 2, 3)]
    sy_cols = pl.ds(pl.multiple_of(zh * 128, 128), 128)
    z_gather = [
        remote(N_ZG + m - 1, sy.at[0, :, sy_cols], sy.at[0, :, sy_cols], at_zh(m))
        for m in (1, 2, 3)
    ]
    g1_right = remote(N_G1, sy.at[0], sy.at[3], at_y(1))
    g1_left = remote(N_G1 + 1, sy.at[0], sy.at[1], at_y(3))
    top, bottom = pl.ds(0, 128), pl.ds(128, 128)
    g2_right = remote(N_G2, sy.at[3, top], sy.at[2, top], at_y(1))
    g2_left = remote(N_G2 + 1, sy.at[1, bottom], sy.at[2, bottom], at_y(3))
    to_core = [remote(N_SY + k, sy.at[k], sp.at[k], core) for k in range(4)]

    load_x = [local(L_X + j, x_hbm.at[:, own_cols(j)], xv.at[j]) for j in range(4)]
    load_x += [local(L_X + 4 + j, x_hbm.at[:, pair_cols(j)], xv.at[4 + j]) for j in range(4)]
    load_c = local(L_C, c_hbm, cv.at[low])
    load_w = local(L_W, w_hbm.at[0], wv.at[0])
    load_fr = [local(L_FR + k, fr_hbm.at[0, :, y_cols(k)], fo.at[k]) for k in range(4)]
    load_op, load_om = local(L_OP, op_hbm, opv), local(L_OM, om_hbm, omv)
    for copy in load_x + [load_c, load_w] + load_fr + [load_op, load_om]:
        copy.start()

    barrier = pltpu.get_barrier_semaphore()
    partners = [pair, core] + [at_x(m) for m in (1, 2, 3)]
    partners += [at_y(1), at_y(3)] + [at_zh(m) for m in (1, 2, 3)]
    for device in partners:
        pl.semaphore_signal(barrier, inc=1, device_id=device, device_id_type=MESH)
    gv[0] = jnp.broadcast_to(gain_ref[...].astype(F32), (8, BLK))
    pl.semaphore_wait(barrier, len(partners))

    for copy in gains:
        copy.start()
    w_right[0].start()
    w_left[1].start()
    cot.start()
    w_right[1].start()
    w_left[0].start()
    for j in (2, 1, 3, 0):
        rows[j].start()
    for k in (2, 1, 3, 0):
        frag[k].start()

    def chunks(count, body, carry=0, size=CH):
        def step(i, held):
            return body(pl.ds(pl.multiple_of(i * size, size), size), held)
        return lax.fori_loop(0, count // size, step, carry)

    def statistics(at, held):
        total = jnp.zeros((CH, BLK), F32)
        for j in range(8):
            value = xv[j, at, :].astype(F32)
            total = total + value * value
        mean = jnp.sum(total, axis=1, keepdims=True) * (1.0 / D)
        inv[0, at, :] = jnp.broadcast_to(lax.rsqrt(mean + 1e-05), (CH, 128))
        return held

    def normalise(j, half):
        source = xv if half == 0 else xp

        def step(at, held):
            unit = source[j, at, :].astype(F32) * wide(inv[half, at, :], BLK // 128)
            rows_at = pl.ds(pl.multiple_of(at.start + half * ROWS, CH), CH)
            nv[j, rows_at, :] = (unit * gv[j, 0:1, :]).astype(BF16)
            return held

        chunks(ROWS, step)

    def add_kv(j, first):
        def step(t, held):
            cols = pl.ds(pl.multiple_of(t * 256, 256), 256)
            part = jnp.dot(nv[j], wv[j, :, cols], preferred_element_type=F32)
            if first:
                kacc[:, cols] = part
            else:
                kacc[:, cols] += part
            return held

        lax.fori_loop(0, KV // 256, step, 0)

    def make_hidden(j):
        def step(t, held):
            at = pl.ds(pl.multiple_of(t * 256, 256), 256)
            hv[j, :, at] = lax.dot_general(
                cv[...], wv[j, at, :], (((1,), (1,)), ((), ())), preferred_element_type=F32
            )
            return held

        lax.fori_loop(0, BLK // 256, step, 0)

    def weight_term(j, half, put):
        def step(t, held):
            cols = pl.ds(pl.multiple_of(t * 512, 512), 512)
            put(cols, lax.dot_general(
                nv[j, :, pl.ds(half * 256, 256)], cv[:, cols], (((0,), (0,)), ((), ())),
                preferred_element_type=F32,
            ))
            return held

        lax.fori_loop(0, KV // 512, step, 0)

    def into(ref, *where):
        def put(cols, value):
            ref[(*where, cols)] = value.astype(ref.dtype)
        return put

    def own_part(zz):
        return pl.ds(pl.multiple_of(zz * 256 + c * 128, 128), 128)

    def pair_sum(k, at, zz):
        cols = own_part(zz)
        return fo[k, at, cols].astype(F32) + fr[k, at, cols].astype(F32)

    for copy in load_x:
        copy.wait()
    chunks(ROWS, statistics)
    for half in range(2):
        part = pl.ds(half * 128, 128)
        inn[0, :, part] = jnp.transpose(inv[0, part, :])[0:8, :]
    inverse.start()

    for k in range(4):
        load_fr[k].wait()
    frag[2].wait_recv()

    def sum_f2(at, held):
        for zz in range(4):
            f2[at, pl.ds(zz * 128, 128)] = pair_sum(2, at, zz).astype(BF16)
        return held

    chunks(256, sum_f2)
    y1_right.start()
    y1_left.start()

    for copy in gains:
        copy.wait_recv()
    for j in (2, 1, 3, 0):
        normalise(j, 0)

    y1_right.wait_recv()
    y1_left.wait_recv()

    def sum_f13(side, k, half):
        def plain(at, held):
            there = pl.ds(pl.multiple_of(at.start + (1 - half) * 128, CH), CH)
            for zz in range(4):
                f13[side, there, pl.ds(zz * 128, 128)] = pair_sum(k, there, zz).astype(BF16)
            return held

        def passing(at, held):
            there = pl.ds(pl.multiple_of(at.start + half * 128, CH), CH)
            for zz in range(4):
                cols = pl.ds(zz * 128, 128)
                total = pair_sum(k, there, zz) + y1r[side, at, cols].astype(F32)
                f13[side, there, cols] = total.astype(BF16)
            return held

        frag[k].wait_recv()
        chunks(128, passing)
        chunks(128, plain)

    sum_f13(0, 1, 0)
    y2_right.start()
    sum_f13(1, 3, 1)
    y2_left.start()

    w_right[0].wait_recv()
    wf_right.start()
    w_left[1].wait_recv()
    wf_left.start()

    load_c.wait()
    load_w.wait()
    cot.wait_recv()
    make_hidden(0)

    frag[0].wait_recv()
    y2_right.wait_recv()
    y2_left.wait_recv()

    def sum_g(m):
        zz = (zh + m) % 4
        cols = pl.ds(pl.multiple_of(zz * 128, 128), 128)

        def step(at, held):
            total = pair_sum(0, at, zz)
            total = total + y2r[0, at, cols].astype(F32) + y2r[1, at, cols].astype(F32)
            if m == 0:
                g0[at, :] = total
            else:
                gb[m, at, :] = total.astype(BF16)
            return held

        chunks(256, step)

    for m in (2, 1, 3):
        sum_g(m)
        z_sum[m - 1].start()
    sum_g(0)

    inverse.wait_recv()
    for half in range(2):
        part = pl.ds(half * 128, 128)
        inv[1, part, :] = jnp.transpose(jnp.broadcast_to(inn[1, 0:1, part], (128, 128)))
    rows[2].wait_recv()
    normalise(2, 1)
    weight_term(2, 0, into(s2, 0, slice(None)))
    s2_right.start()
    weight_term(2, 1, into(s2, 1, slice(None)))
    s2_left.start()

    rows[1].wait_recv()
    normalise(1, 1)
    weight_term(1, 1, into(s1, 0, high))
    s1p_right.start()
    weight_term(1, 0, into(d13, 0, slice(None)))
    rows[3].wait_recv()
    normalise(3, 1)
    weight_term(3, 0, into(s1, 1, low))
    s1p_left.start()
    weight_term(3, 1, into(d13, 1, slice(None)))
    rows[0].wait_recv()
    normalise(0, 1)
    add_kv(0, True)

    w_right[1].wait_recv()
    w_left[0].wait_recv()
    add_kv(1, False)
    add_kv(3, False)

    wf_right.wait_recv()
    wf_left.wait_recv()
    add_kv(2, False)

    def inner_step(half):
        def step(at, held):
            there = pl.ds(pl.multiple_of(at.start + half * ROWS, CH), CH)
            product = jnp.zeros((CH, 256), F32)
            for t in range(4):
                cols = pl.ds(t * 256, 256)
                product = product + cv[there, cols].astype(F32) * kacc[there, cols]
            total = jnp.sum(product, axis=1, keepdims=True) * (1.0 / D)
            inv[2 + half, at, :] = jnp.broadcast_to(total, (CH, 128))
            return held

        chunks(ROWS, step)
        for part in range(2):
            there = pl.ds(half * ROWS + part * 128, 128)
            ins[:, there] = jnp.transpose(inv[2 + half, pl.ds(part * 128, 128), :])[0:8, :]

    inner_step(0)
    inner_step(1)
    inner.start()

    def round_kv(at, held):
        there = pl.ds(pl.multiple_of(at.start + ROWS, CH), CH)
        kvs[at, :] = kacc[there, :].astype(BF16)
        return held

    chunks(ROWS, round_kv)
    kv_half.start()

    for copy in z_sum:
        copy.wait_recv()
    load_op.wait()
    load_om.wait()
    chosen = idx_ref[0]

    def update(at, held):
        total = g0[at, :]
        for m in (1, 2, 3):
            total = total + zr[m, at, :].astype(F32)
        now = opv[chosen, at, :]
        pseudo = now - total * (1.0 / 32.0)
        moment = 0.9 * omv[chosen, at, :] + pseudo
        new = now - 0.7 * (pseudo + 0.9 * moment)
        nm_out[at, :] = moment
        np_out[at, :] = new
        sy[0, at, sy_cols] = new.astype(BF16)
        return held

    chunks(256, update)
    for copy in z_gather:
        copy.start()

    make_hidden(1)
    make_hidden(3)
    make_hidden(2)

    inner.wait_recv()
    for half in range(2):
        for part in range(2):
            mine = pl.ds(half * ROWS + part * 128, 128)
            theirs = pl.ds((1 - half) * ROWS + part * 128, 128)
            total = ins[0:1, mine] + inr[0:1, theirs]
            inv[2 + half, pl.ds(part * 128, 128), :] = jnp.transpose(
                jnp.broadcast_to(total, (128, 128))
            )

    def input_grad(j, half, put):
        source = xv if half == 0 else xp

        def step(at, held):
            there = pl.ds(pl.multiple_of(at.start + half * ROWS, CH), CH)
            scale = wide(inv[half, at, :], BLK // 128)
            unit = source[j, at, :].astype(F32) * scale
            hidden = hv[j, there, :]
            term = (hidden * unit).reshape(CH // 8, 8, BLK)
            scaled = hidden * gv[j, 0:1, :]
            mean = wide(inv[2 + half, at, :], BLK // 128)
            put(at, (scale * (scaled - unit * mean)).astype(BF16))
            return held + jnp.sum(term, axis=0)

        return chunks(ROWS, step, jnp.zeros((8, BLK), F32))

    def put_pair(j):
        def put(at, value):
            dxs[j, at, :] = value
        return put

    def put_own(j):
        def put(at, value):
            dx_out[at, own_cols(j)] = value
        return put

    for j in range(4):
        gs[j] = input_grad(j, 1, put_pair(j))
        dx_half[j].start()

    def add_passing(side, first_row):
        def step(at, held):
            there = pl.ds(pl.multiple_of(at.start + first_row, CH), CH)
            s1[side, there, :] = (d13[side, at, :] + s2r[side, at, :].astype(F32)).astype(BF16)
            return held
        chunks(256, step)

    s2_right.wait_recv()
    add_passing(0, 0)
    s1s_right.start()
    s2_left.wait_recv()
    add_passing(1, 256)
    s1s_left.start()

    for copy in z_gather:
        copy.wait_recv()
    g1_right.start()
    g1_left.start()
    to_core[0].start()

    for j in (1, 2, 3, 0):
        total = gs[j] + input_grad(j, 0, put_own(j))
        gs[j] = jnp.broadcast_to(jnp.sum(total, axis=0, keepdims=True), (8, BLK))
        if j > 0:
            gain_sum[j - 1].start()

    g1_right.wait_recv()
    g2_right.start()
    g1_left.wait_recv()
    g2_left.start()
    to_core[3].start()
    to_core[1].start()

    weight_term(0, 0, into(d0, low))
    weight_term(0, 1, into(d0, high))

    def place(k):
        to_core[k].wait_recv()
        first = ((y + k) % 4) * 1024

        def step(at, held):
            for zz in range(4):
                cols = pl.ds(zz * 128, 128)
                mine = pl.ds(pl.multiple_of(first + zz * 256 + c * 128, 128), 128)
                theirs = pl.ds(pl.multiple_of(first + zz * 256 + (1 - c) * 128, 128), 128)
                sy_out[at, mine] = sy[k, at, cols]
                sy_out[at, theirs] = sp[k, at, cols]
            return held

        chunks(256, step)

    place(0)
    g2_right.wait_recv()
    g2_left.wait_recv()
    to_core[2].start()
    place(3)
    place(1)

    kv_half.wait_recv()

    def finish_kv(at, held):
        kv_out[at, :] = (kacc[at, :] + kvr[at, :].astype(F32)).astype(BF16)
        return held

    chunks(ROWS, finish_kv)
    place(2)
    for copy in gain_sum:
        copy.wait_recv()
    dg_out[...] = gs[0] + gr[1] + gr[2] + gr[3]
    for copy in (s1p_right, s1p_left, s1s_right, s1s_left):
        copy.wait_recv()

    def finish_dw(at, held):
        total = d0[at, :] + s1r[0, at, :].astype(F32) + s1r[1, at, :].astype(F32)
        dw_out[at, :] = total.astype(BF16)
        return held

    chunks(BLK, finish_dw)
    for copy in dx_half:
        copy.wait_recv()

    for copy in (
        w_right + w_left + [cot, wf_right, wf_left, inverse, s2_right, s2_left]
        + [s1p_right, s1p_left, s1s_right, s1s_left, inner, kv_half]
        + [y1_right, y1_left, y2_right, y2_left, g1_right, g1_left, g2_right, g2_left]
        + rows + gains + dx_half + gain_sum + frag + z_sum + z_gather + to_core
    ):
        copy.wait_send()


def store(kv, dx, dw, dg, np_, nm, sy, kv_out, dx_out, dw_out, dg_out, np_out, nm_out, sy_out, sem):
    copies = [
        pltpu.make_async_copy(source, target, sem.at[i])
        for i, (source, target) in enumerate(
            ((dx, dx_out), (sy, sy_out), (dw, dw_out.at[0]), (kv, kv_out), (np_, np_out), (nm, nm_out))
        )
    ]
    for copy in copies:
        copy.start()
    dg_out[...] = dg[0:1, :].astype(BF16)
    for copy in copies:
        copy.wait()


def on_device(x, gain, w, cot, frag, params, moment, index):
    any_spec = pl.BlockSpec(memory_space=pl.ANY)
    vmem = pl.BlockSpec(memory_space=pltpu.VMEM)
    out = jax.ShapeDtypeStruct
    held = pl.pallas_call(
        kernel,
        out_shape=(
            pltpu.VMEM((ROWS, KV), BF16), pltpu.VMEM((ROWS, D), BF16), pltpu.VMEM((BLK, KV), BF16),
            pltpu.VMEM((8, BLK), F32), pltpu.VMEM((256, 128), F32), pltpu.VMEM((256, 128), F32),
            pltpu.VMEM((256, D), BF16),
        ),
        in_specs=[any_spec, vmem] + [any_spec] * 5 + [pl.BlockSpec(memory_space=pltpu.SMEM)],
        out_specs=(vmem,) * 7,
        scratch_shapes=[
            pltpu.VMEM((8, ROWS, BLK), BF16),
            pltpu.VMEM((4, ROWS, BLK), BF16),
            pltpu.VMEM((2 * ROWS, KV), BF16),
            pltpu.VMEM((4, BLK, KV), BF16),
            pltpu.VMEM((4, 8, BLK), F32),
            pltpu.VMEM((4, ROWS, 128), F32),
            pltpu.VMEM((4, 2 * ROWS, BLK), BF16),
            pltpu.VMEM((4, 2 * ROWS, BLK), F32),
            pltpu.VMEM((2 * ROWS, KV), F32),
            pltpu.VMEM((BLK, KV), F32),
            pltpu.VMEM((2, 256, KV), F32),
            pltpu.VMEM((2, 256, KV), BF16),
            pltpu.VMEM((2, 256, KV), BF16),
            pltpu.VMEM((2, BLK, KV), BF16),
            pltpu.VMEM((2, BLK, KV), BF16),
            pltpu.VMEM((2, 8, ROWS), F32),
            pltpu.VMEM((8, 2 * ROWS), F32),
            pltpu.VMEM((8, 2 * ROWS), F32),
            pltpu.VMEM((ROWS, KV), BF16),
            pltpu.VMEM((ROWS, KV), BF16),
            pltpu.VMEM((4, ROWS, BLK), BF16),
            pltpu.VMEM((4, 8, BLK), F32),
            pltpu.VMEM((4, 8, BLK), F32),
            pltpu.VMEM((4, 256, 1024), BF16),
            pltpu.VMEM((4, 256, 1024), BF16),
            pltpu.VMEM((256, 512), BF16),
            pltpu.VMEM((2, 128, 512), BF16),
            pltpu.VMEM((2, 256, 512), BF16),
            pltpu.VMEM((2, 256, 512), BF16),
            pltpu.VMEM((4, 256, 128), BF16),
            pltpu.VMEM((256, 128), F32),
            pltpu.VMEM((4, 256, 128), BF16),
            pltpu.VMEM((4, 256, 128), F32),
            pltpu.VMEM((4, 256, 128), F32),
            pltpu.VMEM((4, 256, 512), BF16),
            pltpu.VMEM((4, 256, 512), BF16),
            pltpu.SemaphoreType.DMA((N_REMOTE,)),
            pltpu.SemaphoreType.DMA((N_REMOTE,)),
            pltpu.SemaphoreType.DMA((N_LOCAL,)),
        ],
        compiler_params=pltpu.CompilerParams(
            collective_id=0, has_side_effects=True, vmem_limit_bytes=52 * 1024 * 1024
        ),
        cost_estimate=pl.CostEstimate(
            flops=6 * ROWS * D * KV, bytes_accessed=24 << 20, transcendentals=ROWS
        ),
    )(x, gain, w, cot, frag, params, moment, index)
    return pl.pallas_call(
        store,
        out_shape=(
            out((ROWS, KV), BF16), out((ROWS, D), BF16), out((1, BLK, KV), BF16),
            out((1, BLK), BF16), out((256, 128), F32), out((256, 128), F32),
            out((256, D), BF16),
        ),
        in_specs=[vmem] * 7,
        out_specs=(any_spec, any_spec, any_spec, vmem, any_spec, any_spec, any_spec),
        scratch_shapes=[pltpu.SemaphoreType.DMA((6,))],
    )(*held)


def solution(mesh):
    return jax.shard_map(
        on_device,
        mesh=mesh,
        in_specs=(
            P(("rep", "fsdp"), None),
            P("rep", "fsdp"),
            P("rep", "fsdp", None),
            P(("rep", "fsdp"), None),
            P("rep", "fsdp", None),
            P(None, "fsdp", "rep"),
            P(None, "fsdp", "rep"),
            P(),
        ),
        out_specs=(
            P(("rep", "fsdp"), None),
            P(("rep", "fsdp"), None),
            P("rep", "fsdp", None),
            P("rep", "fsdp"),
            P("fsdp", "rep"),
            P("fsdp", "rep"),
            P("fsdp", None),
        ),
        check_vma=False,
    )
```

```python
import jax
import jax.numpy as jnp
from jax import lax
from jax.experimental import pallas as pl
from jax.experimental.pallas import tpu as pltpu
from jax.sharding import PartitionSpec as P

MESH = pl.DeviceIdType.MESH
F32, BF16 = jnp.float32, jnp.bfloat16
D = 4096
ROWS = 256
BLK = 512
KV = 1024
CH = 32

N_COT, N_X, N_W, N_GAIN, N_INV = 0, 1, 5, 9, 12
N_WF = 50
N_S2, N_S1P, N_S1S, N_INNER, N_KV, N_DX, N_GG = 13, 15, 17, 19, 20, 21, 25
N_FR, N_Y1, N_Y2, N_Z, N_ZG, N_G1, N_G2, N_SY = 28, 32, 34, 36, 39, 42, 44, 46
N_REMOTE = 52
L_X, L_C, L_W, L_FR, L_OP, L_OM = 0, 8, 9, 10, 14, 15
N_LOCAL = 16


def wide(value, times):
    return jnp.concatenate([value] * times, axis=1)


def kernel(
    x_hbm, gain_ref, w_hbm, c_hbm, fr_hbm, op_hbm, om_hbm, idx_ref,
    kv_out, dx_out, dw_out, dg_out, np_out, nm_out, sy_out,
    xv, xp, cv, wv, gv, inv, nv, hv, kacc, d0, d13, s2, s2r, s1, s1r,
    inn, ins, inr, kvs, kvr, dxs, gs, gr,
    fo, fr, f2, y1r, f13, y2r, gb, g0, zr, opv, omv, sy, sp,
    ssem, rsem, lsem,
):
    f, r = lax.axis_index("fsdp"), lax.axis_index("rep")
    x, z = f // 2, f % 2
    y, zh, c = r // 8, (r // 2) % 4, r % 2

    def at_x(step):
        return {"fsdp": ((x + step) % 4) * 2 + z}

    def at_y(step):
        return {"rep": ((y + step) % 4) * 8 + zh * 2 + c}

    def at_zh(step):
        return {"rep": y * 8 + ((zh + step) % 4) * 2 + c}

    pair, core = {"fsdp": x * 2 + 1 - z}, {"rep": y * 8 + zh * 2 + 1 - c}

    def remote(number, source, target, device):
        return pltpu.make_async_remote_copy(
            src_ref=source, dst_ref=target, send_sem=ssem.at[number], recv_sem=rsem.at[number],
            device_id=device, device_id_type=MESH,
        )

    def local(number, source, target):
        return pltpu.make_async_copy(source, target, lsem.at[number])

    def own_cols(j):
        return pl.ds(pl.multiple_of((((x + j) % 4) * 2 + z) * BLK, BLK), BLK)

    def pair_cols(j):
        return pl.ds(pl.multiple_of((((x + j) % 4) * 2 + 1 - z) * BLK, BLK), BLK)

    def y_cols(k):
        return pl.ds(pl.multiple_of(((y + k) % 4) * 1024, 1024), 1024)

    low, high = pl.ds(0, ROWS), pl.ds(ROWS, ROWS)

    cot = remote(N_COT, c_hbm, cv.at[high], pair)
    rows = [remote(N_X + j, x_hbm.at[:, pair_cols(j)], xp.at[j], pair) for j in range(4)]
    parts = (low, high)
    w_right = [remote(N_W + h, w_hbm.at[0, parts[h]], wv.at[3, parts[h]], at_x(1)) for h in range(2)]
    w_left = [remote(N_W + 2 + h, w_hbm.at[0, parts[h]], wv.at[1, parts[h]], at_x(3)) for h in range(2)]
    wf_right = remote(N_WF, wv.at[3, low], wv.at[2, low], at_x(1))
    wf_left = remote(N_WF + 1, wv.at[1, high], wv.at[2, high], at_x(3))
    gains = [remote(N_GAIN + m - 1, gv.at[0], gv.at[4 - m], at_x(m)) for m in (1, 2, 3)]
    inverse = remote(N_INV, inn.at[0], inn.at[1], pair)
    s2_right = remote(N_S2, s2.at[0], s2r.at[0], at_x(1))
    s2_left = remote(N_S2 + 1, s2.at[1], s2r.at[1], at_x(3))
    s1p_right = remote(N_S1P, s1.at[0, high], s1r.at[0, high], at_x(1))
    s1p_left = remote(N_S1P + 1, s1.at[1, low], s1r.at[1, low], at_x(3))
    s1s_right = remote(N_S1S, s1.at[0, low], s1r.at[0, low], at_x(1))
    s1s_left = remote(N_S1S + 1, s1.at[1, high], s1r.at[1, high], at_x(3))
    inner = remote(N_INNER, ins, inr, pair)
    kv_half = remote(N_KV, kvs, kvr, pair)
    dx_half = [remote(N_DX + j, dxs.at[j], dx_out.at[:, own_cols(j)], pair) for j in range(4)]
    gain_sum = [remote(N_GG + m - 1, gs.at[m], gr.at[m], at_x(m)) for m in (1, 2, 3)]
    frag = [remote(N_FR + k, fr_hbm.at[0, :, y_cols(k)], fr.at[k], core) for k in range(4)]
    y1_right = remote(N_Y1, f2.at[pl.ds(0, 128)], y1r.at[0], at_y(1))
    y1_left = remote(N_Y1 + 1, f2.at[pl.ds(128, 128)], y1r.at[1], at_y(3))
    y2_right = remote(N_Y2, f13.at[0], y2r.at[0], at_y(1))
    y2_left = remote(N_Y2 + 1, f13.at[1], y2r.at[1], at_y(3))
    z_sum = [remote(N_Z + m - 1, gb.at[m], zr.at[m], at_zh(m)) for m in (1, 2, 3)]
    sy_cols = pl.ds(pl.multiple_of(zh * 128, 128), 128)
    z_gather = [
        remote(N_ZG + m - 1, sy.at[0, :, sy_cols], sy.at[0, :, sy_cols], at_zh(m))
        for m in (1, 2, 3)
    ]
    g1_right = remote(N_G1, sy.at[0], sy.at[3], at_y(1))
    g1_left = remote(N_G1 + 1, sy.at[0], sy.at[1], at_y(3))
    top, bottom = pl.ds(0, 128), pl.ds(128, 128)
    g2_right = remote(N_G2, sy.at[3, top], sy.at[2, top], at_y(1))
    g2_left = remote(N_G2 + 1, sy.at[1, bottom], sy.at[2, bottom], at_y(3))
    to_core = [remote(N_SY + k, sy.at[k], sp.at[k], core) for k in range(4)]

    load_x = [local(L_X + j, x_hbm.at[:, own_cols(j)], xv.at[j]) for j in range(4)]
    load_x += [local(L_X + 4 + j, x_hbm.at[:, pair_cols(j)], xv.at[4 + j]) for j in range(4)]
    load_c = local(L_C, c_hbm, cv.at[low])
    load_w = local(L_W, w_hbm.at[0], wv.at[0])
    load_fr = [local(L_FR + k, fr_hbm.at[0, :, y_cols(k)], fo.at[k]) for k in range(4)]
    load_op, load_om = local(L_OP, op_hbm, opv), local(L_OM, om_hbm, omv)
    for copy in load_x + [load_c, load_w] + load_fr + [load_op, load_om]:
        copy.start()

    barrier = pltpu.get_barrier_semaphore()
    partners = [pair, core] + [at_x(m) for m in (1, 2, 3)]
    partners += [at_y(1), at_y(3)] + [at_zh(m) for m in (1, 2, 3)]
    for device in partners:
        pl.semaphore_signal(barrier, inc=1, device_id=device, device_id_type=MESH)
    gv[0] = jnp.broadcast_to(gain_ref[...].astype(F32), (8, BLK))
    pl.semaphore_wait(barrier, len(partners))

    for copy in gains:
        copy.start()
    w_right[0].start()
    w_left[1].start()
    cot.start()
    w_right[1].start()
    w_left[0].start()
    rows[2].start()
    for k in (2, 1, 3, 0):
        frag[k].start()

    def chunks(count, body, carry=0, size=CH):
        def step(i, held):
            return body(pl.ds(pl.multiple_of(i * size, size), size), held)
        return lax.fori_loop(0, count // size, step, carry)

    def statistics(at, held):
        total = jnp.zeros((CH, BLK), F32)
        for j in range(8):
            value = xv[j, at, :].astype(F32)
            total = total + value * value
        mean = jnp.sum(total, axis=1, keepdims=True) * (1.0 / D)
        inv[0, at, :] = jnp.broadcast_to(lax.rsqrt(mean + 1e-05), (CH, 128))
        return held

    def normalise(j, half):
        source = xv if half == 0 else xp

        def step(at, held):
            unit = source[j, at, :].astype(F32) * wide(inv[half, at, :], BLK // 128)
            rows_at = pl.ds(pl.multiple_of(at.start + half * ROWS, CH), CH)
            nv[j, rows_at, :] = (unit * gv[j, 0:1, :]).astype(BF16)
            return held

        chunks(ROWS, step)

    def add_kv(j, first):
        def step(t, held):
            cols = pl.ds(pl.multiple_of(t * 256, 256), 256)
            part = jnp.dot(nv[j], wv[j, :, cols], preferred_element_type=F32)
            if first:
                kacc[:, cols] = part
            else:
                kacc[:, cols] += part
            return held

        lax.fori_loop(0, KV // 256, step, 0)

    def make_hidden(j):
        def step(t, held):
            at = pl.ds(pl.multiple_of(t * 256, 256), 256)
            hv[j, :, at] = lax.dot_general(
                cv[...], wv[j, at, :], (((1,), (1,)), ((), ())), preferred_element_type=F32
            )
            return held

        lax.fori_loop(0, BLK // 256, step, 0)

    def weight_term(j, half, put):
        def step(t, held):
            cols = pl.ds(pl.multiple_of(t * 512, 512), 512)
            put(cols, lax.dot_general(
                nv[j, :, pl.ds(half * 256, 256)], cv[:, cols], (((0,), (0,)), ((), ())),
                preferred_element_type=F32,
            ))
            return held

        lax.fori_loop(0, KV // 512, step, 0)

    def into(ref, *where):
        def put(cols, value):
            ref[(*where, cols)] = value.astype(ref.dtype)
        return put

    def own_part(zz):
        return pl.ds(pl.multiple_of(zz * 256 + c * 128, 128), 128)

    def pair_sum(k, at, zz):
        cols = own_part(zz)
        return fo[k, at, cols].astype(F32) + fr[k, at, cols].astype(F32)

    for copy in load_x:
        copy.wait()
    chunks(ROWS, statistics)
    for half in range(2):
        part = pl.ds(half * 128, 128)
        inn[0, :, part] = jnp.transpose(inv[0, part, :])[0:8, :]
    inverse.start()

    for k in range(4):
        load_fr[k].wait()
    frag[2].wait_recv()

    def sum_f2(at, held):
        for zz in range(4):
            f2[at, pl.ds(zz * 128, 128)] = pair_sum(2, at, zz).astype(BF16)
        return held

    chunks(256, sum_f2)
    y1_right.start()
    y1_left.start()

    for copy in gains:
        copy.wait_recv()
    for j in (2, 1, 3, 0):
        normalise(j, 0)

    y1_right.wait_recv()
    y1_left.wait_recv()

    def sum_f13(side, k, half):
        def plain(at, held):
            there = pl.ds(pl.multiple_of(at.start + (1 - half) * 128, CH), CH)
            for zz in range(4):
                f13[side, there, pl.ds(zz * 128, 128)] = pair_sum(k, there, zz).astype(BF16)
            return held

        def passing(at, held):
            there = pl.ds(pl.multiple_of(at.start + half * 128, CH), CH)
            for zz in range(4):
                cols = pl.ds(zz * 128, 128)
                total = pair_sum(k, there, zz) + y1r[side, at, cols].astype(F32)
                f13[side, there, cols] = total.astype(BF16)
            return held

        frag[k].wait_recv()
        chunks(128, passing)
        chunks(128, plain)

    sum_f13(0, 1, 0)
    y2_right.start()
    sum_f13(1, 3, 1)
    y2_left.start()

    w_right[0].wait_recv()
    wf_right.start()
    w_left[1].wait_recv()
    wf_left.start()

    load_c.wait()
    load_w.wait()
    cot.wait_recv()
    cot.wait_send()
    rows[1].start()
    make_hidden(0)

    frag[0].wait_recv()
    y2_right.wait_recv()
    y2_left.wait_recv()

    def sum_g(m):
        zz = (zh + m) % 4
        cols = pl.ds(pl.multiple_of(zz * 128, 128), 128)

        def step(at, held):
            total = pair_sum(0, at, zz)
            total = total + y2r[0, at, cols].astype(F32) + y2r[1, at, cols].astype(F32)
            if m == 0:
                g0[at, :] = total
            else:
                gb[m, at, :] = total.astype(BF16)
            return held

        chunks(256, step)

    for m in (2, 1, 3):
        sum_g(m)
        z_sum[m - 1].start()
    sum_g(0)

    inverse.wait_recv()
    for half in range(2):
        part = pl.ds(half * 128, 128)
        inv[1, part, :] = jnp.transpose(jnp.broadcast_to(inn[1, 0:1, part], (128, 128)))
    rows[2].wait_recv()
    rows[2].wait_send()
    rows[3].start()
    normalise(2, 1)
    weight_term(2, 0, into(s2, 0, slice(None)))
    s2_right.start()
    weight_term(2, 1, into(s2, 1, slice(None)))
    s2_left.start()

    rows[1].wait_recv()
    rows[1].wait_send()
    rows[0].start()
    normalise(1, 1)
    weight_term(1, 1, into(s1, 0, high))
    s1p_right.start()
    weight_term(1, 0, into(d13, 0, slice(None)))

    for copy in z_sum:
        copy.wait_recv()
    load_op.wait()
    load_om.wait()
    chosen = idx_ref[0]

    def update(at, held):
        total = g0[at, :]
        for m in (1, 2, 3):
            total = total + zr[m, at, :].astype(F32)
        now = opv[chosen, at, :]
        pseudo = now - total * (1.0 / 32.0)
        moment = 0.9 * omv[chosen, at, :] + pseudo
        new = now - 0.7 * (pseudo + 0.9 * moment)
        nm_out[at, :] = moment
        np_out[at, :] = new
        sy[0, at, sy_cols] = new.astype(BF16)
        return held

    chunks(256, update)
    for copy in z_gather:
        copy.start()

    rows[3].wait_recv()
    normalise(3, 1)
    weight_term(3, 0, into(s1, 1, low))
    s1p_left.start()
    weight_term(3, 1, into(d13, 1, slice(None)))

    w_right[1].wait_recv()
    w_left[0].wait_recv()
    add_kv(1, True)
    add_kv(3, False)
    wf_right.wait_recv()
    wf_left.wait_recv()
    add_kv(2, False)
    rows[0].wait_recv()
    normalise(0, 1)
    add_kv(0, False)

    def inner_step(half):
        def step(at, held):
            there = pl.ds(pl.multiple_of(at.start + half * ROWS, CH), CH)
            product = jnp.zeros((CH, 256), F32)
            for t in range(4):
                cols = pl.ds(t * 256, 256)
                product = product + cv[there, cols].astype(F32) * kacc[there, cols]
            total = jnp.sum(product, axis=1, keepdims=True) * (1.0 / D)
            inv[2 + half, at, :] = jnp.broadcast_to(total, (CH, 128))
            return held

        chunks(ROWS, step)
        for part in range(2):
            there = pl.ds(half * ROWS + part * 128, 128)
            ins[:, there] = jnp.transpose(inv[2 + half, pl.ds(part * 128, 128), :])[0:8, :]

    inner_step(0)
    inner_step(1)
    inner.start()

    def round_kv(at, held):
        there = pl.ds(pl.multiple_of(at.start + ROWS, CH), CH)
        kvs[at, :] = kacc[there, :].astype(BF16)
        return held

    chunks(ROWS, round_kv)
    kv_half.start()
    make_hidden(1)
    make_hidden(3)
    make_hidden(2)

    def add_passing(side, first_row):
        def step(at, held):
            there = pl.ds(pl.multiple_of(at.start + first_row, CH), CH)
            s1[side, there, :] = (d13[side, at, :] + s2r[side, at, :].astype(F32)).astype(BF16)
            return held
        chunks(256, step)

    s2_right.wait_recv()
    add_passing(0, 0)
    s1s_right.start()
    s2_left.wait_recv()
    add_passing(1, 256)
    s1s_left.start()

    for copy in z_gather:
        copy.wait_recv()
    g1_right.start()
    g1_left.start()
    to_core[0].start()

    inner.wait_recv()
    for half in range(2):
        for part in range(2):
            mine = pl.ds(half * ROWS + part * 128, 128)
            theirs = pl.ds((1 - half) * ROWS + part * 128, 128)
            total = ins[0:1, mine] + inr[0:1, theirs]
            inv[2 + half, pl.ds(part * 128, 128), :] = jnp.transpose(
                jnp.broadcast_to(total, (128, 128))
            )

    def input_grad(j, half, put):
        source = xv if half == 0 else xp

        def step(at, held):
            there = pl.ds(pl.multiple_of(at.start + half * ROWS, CH), CH)
            scale = wide(inv[half, at, :], BLK // 128)
            unit = source[j, at, :].astype(F32) * scale
            hidden = hv[j, there, :]
            term = (hidden * unit).reshape(CH // 8, 8, BLK)
            scaled = hidden * gv[j, 0:1, :]
            mean = wide(inv[2 + half, at, :], BLK // 128)
            put(at, (scale * (scaled - unit * mean)).astype(BF16))
            return held + jnp.sum(term, axis=0)

        return chunks(ROWS, step, jnp.zeros((8, BLK), F32))

    def put_pair(j):
        def put(at, value):
            dxs[j, at, :] = value
        return put

    def put_own(j):
        def put(at, value):
            dx_out[at, own_cols(j)] = value
        return put

    for j in range(4):
        gs[j] = input_grad(j, 1, put_pair(j))
        dx_half[j].start()

    for j in (1, 2, 3, 0):
        total = gs[j] + input_grad(j, 0, put_own(j))
        gs[j] = jnp.broadcast_to(jnp.sum(total, axis=0, keepdims=True), (8, BLK))
        if j > 0:
            gain_sum[j - 1].start()

    g1_right.wait_recv()
    g2_right.start()
    g1_left.wait_recv()
    g2_left.start()
    to_core[3].start()
    to_core[1].start()

    weight_term(0, 0, into(d0, low))
    weight_term(0, 1, into(d0, high))

    def place(k):
        to_core[k].wait_recv()
        first = ((y + k) % 4) * 1024

        def step(at, held):
            for zz in range(4):
                cols = pl.ds(zz * 128, 128)
                mine = pl.ds(pl.multiple_of(first + zz * 256 + c * 128, 128), 128)
                theirs = pl.ds(pl.multiple_of(first + zz * 256 + (1 - c) * 128, 128), 128)
                sy_out[at, mine] = sy[k, at, cols]
                sy_out[at, theirs] = sp[k, at, cols]
            return held

        chunks(256, step)

    place(0)
    g2_right.wait_recv()
    g2_left.wait_recv()
    to_core[2].start()
    place(3)
    place(1)

    kv_half.wait_recv()

    def finish_kv(at, held):
        kv_out[at, :] = (kacc[at, :] + kvr[at, :].astype(F32)).astype(BF16)
        return held

    chunks(ROWS, finish_kv)
    place(2)
    for copy in gain_sum:
        copy.wait_recv()
    dg_out[...] = gs[0] + gr[1] + gr[2] + gr[3]
    for copy in (s1p_right, s1p_left, s1s_right, s1s_left):
        copy.wait_recv()

    def finish_dw(at, held):
        total = d0[at, :] + s1r[0, at, :].astype(F32) + s1r[1, at, :].astype(F32)
        dw_out[at, :] = total.astype(BF16)
        return held

    chunks(BLK, finish_dw)
    for copy in dx_half:
        copy.wait_recv()

    for copy in (
        w_right + w_left + [rows[3], rows[0], wf_right, wf_left, inverse, s2_right, s2_left]
        + [s1p_right, s1p_left, s1s_right, s1s_left, inner, kv_half]
        + [y1_right, y1_left, y2_right, y2_left, g1_right, g1_left, g2_right, g2_left]
        + gains + dx_half + gain_sum + frag + z_sum + z_gather + to_core
    ):
        copy.wait_send()


def store(kv, dx, dw, dg, np_, nm, sy, kv_out, dx_out, dw_out, dg_out, np_out, nm_out, sy_out, sem):
    copies = [
        pltpu.make_async_copy(source, target, sem.at[i])
        for i, (source, target) in enumerate(
            ((dx, dx_out), (sy, sy_out), (dw, dw_out.at[0]), (kv, kv_out), (np_, np_out), (nm, nm_out))
        )
    ]
    for copy in copies:
        copy.start()
    dg_out[...] = dg[0:1, :].astype(BF16)
    for copy in copies:
        copy.wait()


def on_device(x, gain, w, cot, frag, params, moment, index):
    any_spec = pl.BlockSpec(memory_space=pl.ANY)
    vmem = pl.BlockSpec(memory_space=pltpu.VMEM)
    out = jax.ShapeDtypeStruct
    held = pl.pallas_call(
        kernel,
        out_shape=(
            pltpu.VMEM((ROWS, KV), BF16), pltpu.VMEM((ROWS, D), BF16), pltpu.VMEM((BLK, KV), BF16),
            pltpu.VMEM((8, BLK), F32), pltpu.VMEM((256, 128), F32), pltpu.VMEM((256, 128), F32),
            pltpu.VMEM((256, D), BF16),
        ),
        in_specs=[any_spec, vmem] + [any_spec] * 5 + [pl.BlockSpec(memory_space=pltpu.SMEM)],
        out_specs=(vmem,) * 7,
        scratch_shapes=[
            pltpu.VMEM((8, ROWS, BLK), BF16),
            pltpu.VMEM((4, ROWS, BLK), BF16),
            pltpu.VMEM((2 * ROWS, KV), BF16),
            pltpu.VMEM((4, BLK, KV), BF16),
            pltpu.VMEM((4, 8, BLK), F32),
            pltpu.VMEM((4, ROWS, 128), F32),
            pltpu.VMEM((4, 2 * ROWS, BLK), BF16),
            pltpu.VMEM((4, 2 * ROWS, BLK), F32),
            pltpu.VMEM((2 * ROWS, KV), F32),
            pltpu.VMEM((BLK, KV), F32),
            pltpu.VMEM((2, 256, KV), F32),
            pltpu.VMEM((2, 256, KV), BF16),
            pltpu.VMEM((2, 256, KV), BF16),
            pltpu.VMEM((2, BLK, KV), BF16),
            pltpu.VMEM((2, BLK, KV), BF16),
            pltpu.VMEM((2, 8, ROWS), F32),
            pltpu.VMEM((8, 2 * ROWS), F32),
            pltpu.VMEM((8, 2 * ROWS), F32),
            pltpu.VMEM((ROWS, KV), BF16),
            pltpu.VMEM((ROWS, KV), BF16),
            pltpu.VMEM((4, ROWS, BLK), BF16),
            pltpu.VMEM((4, 8, BLK), F32),
            pltpu.VMEM((4, 8, BLK), F32),
            pltpu.VMEM((4, 256, 1024), BF16),
            pltpu.VMEM((4, 256, 1024), BF16),
            pltpu.VMEM((256, 512), BF16),
            pltpu.VMEM((2, 128, 512), BF16),
            pltpu.VMEM((2, 256, 512), BF16),
            pltpu.VMEM((2, 256, 512), BF16),
            pltpu.VMEM((4, 256, 128), BF16),
            pltpu.VMEM((256, 128), F32),
            pltpu.VMEM((4, 256, 128), BF16),
            pltpu.VMEM((4, 256, 128), F32),
            pltpu.VMEM((4, 256, 128), F32),
            pltpu.VMEM((4, 256, 512), BF16),
            pltpu.VMEM((4, 256, 512), BF16),
            pltpu.SemaphoreType.DMA((N_REMOTE,)),
            pltpu.SemaphoreType.DMA((N_REMOTE,)),
            pltpu.SemaphoreType.DMA((N_LOCAL,)),
        ],
        compiler_params=pltpu.CompilerParams(
            collective_id=0, has_side_effects=True, vmem_limit_bytes=52 * 1024 * 1024
        ),
        cost_estimate=pl.CostEstimate(
            flops=6 * ROWS * D * KV, bytes_accessed=24 << 20, transcendentals=ROWS
        ),
    )(x, gain, w, cot, frag, params, moment, index)
    return pl.pallas_call(
        store,
        out_shape=(
            out((ROWS, KV), BF16), out((ROWS, D), BF16), out((1, BLK, KV), BF16),
            out((1, BLK), BF16), out((256, 128), F32), out((256, 128), F32),
            out((256, D), BF16),
        ),
        in_specs=[vmem] * 7,
        out_specs=(any_spec, any_spec, any_spec, vmem, any_spec, any_spec, any_spec),
        scratch_shapes=[pltpu.SemaphoreType.DMA((6,))],
        compiler_params=pltpu.CompilerParams(vmem_limit_bytes=2 * 1024 * 1024),
    )(*held)


def solution(mesh):
    return jax.shard_map(
        on_device,
        mesh=mesh,
        in_specs=(
            P(("rep", "fsdp"), None),
            P("rep", "fsdp"),
            P("rep", "fsdp", None),
            P(("rep", "fsdp"), None),
            P("rep", "fsdp", None),
            P(None, "fsdp", "rep"),
            P(None, "fsdp", "rep"),
            P(),
        ),
        out_specs=(
            P(("rep", "fsdp"), None),
            P(("rep", "fsdp"), None),
            P("rep", "fsdp", None),
            P("rep", "fsdp"),
            P("fsdp", "rep"),
            P("fsdp", "rep"),
            P("fsdp", None),
        ),
        check_vma=False,
    )
```

```python
import jax
import jax.numpy as jnp
from jax import lax
from jax.experimental import pallas as pl
from jax.experimental.pallas import tpu as pltpu
from jax.sharding import PartitionSpec as P

MESH = pl.DeviceIdType.MESH
F32, BF16 = jnp.float32, jnp.bfloat16
D = 4096
ROWS = 256
BLK = 512
KV = 1024
CH = 32

N_COT, N_X, N_W, N_GAIN, N_INV = 0, 1, 5, 9, 12
N_WF, N_KV1, N_Z2, N_ZG2 = 50, 52, 53, 55
N_S2, N_S1P, N_S1S, N_INNER, N_KV, N_DX, N_GG = 13, 15, 17, 19, 20, 21, 25
N_FR, N_Y1, N_Y2, N_Z1, N_ZG1, N_G1, N_G2, N_SY = 28, 32, 34, 36, 39, 42, 44, 46
N_REMOTE = 57
L_X, L_C, L_W, L_FR, L_OP, L_OM, L_IDX = 0, 8, 9, 10, 14, 15, 16
N_LOCAL = 17


def wide(value, times):
    return jnp.concatenate([value] * times, axis=1)


def kernel(
    x_hbm, gain_ref, w_hbm, c_hbm, fr_hbm, op_hbm, om_hbm, idx_hbm,
    kv_out, dx_out, dw_out, dg_out, np_out, nm_out, sy_out,
    xv, xp, cv, wv, gv, inv, nv, hv, kacc, d0, d13, s2, s2r, s1, s1r,
    inn, ins, inr, kvs, kvr, dxs, gs, gr,
    fo, fr, f2, y1r, f13, y2r, gb, g0, z1r, zr, opv, omv, sy, sp, idx_ref,
    ssem, rsem, lsem,
):
    f, r = lax.axis_index("fsdp"), lax.axis_index("rep")
    x, z = f // 2, f % 2
    y, zh, c = r // 8, (r // 2) % 4, r % 2

    def at_x(step):
        return {"fsdp": ((x + step) % 4) * 2 + z}

    def at_y(step):
        return {"rep": ((y + step) % 4) * 8 + zh * 2 + c}

    def at_zh(step):
        return {"rep": y * 8 + ((zh + step) % 4) * 2 + c}

    pair, core = {"fsdp": x * 2 + 1 - z}, {"rep": y * 8 + zh * 2 + 1 - c}

    def remote(number, source, target, device):
        return pltpu.make_async_remote_copy(
            src_ref=source, dst_ref=target, send_sem=ssem.at[number], recv_sem=rsem.at[number],
            device_id=device, device_id_type=MESH,
        )

    def local(number, source, target):
        return pltpu.make_async_copy(source, target, lsem.at[number])

    def own_cols(j):
        return pl.ds(pl.multiple_of((((x + j) % 4) * 2 + z) * BLK, BLK), BLK)

    def pair_cols(j):
        return pl.ds(pl.multiple_of((((x + j) % 4) * 2 + 1 - z) * BLK, BLK), BLK)

    def y_cols(k):
        return pl.ds(pl.multiple_of(((y + k) % 4) * 1024, 1024), 1024)

    low, high = pl.ds(0, ROWS), pl.ds(ROWS, ROWS)

    cot = remote(N_COT, c_hbm, cv.at[high], pair)
    rows = [remote(N_X + j, x_hbm.at[:, pair_cols(j)], xp.at[j], pair) for j in range(4)]
    parts = (low, high)
    w_right = [remote(N_W + h, w_hbm.at[0, parts[h]], wv.at[3, parts[h]], at_x(1)) for h in range(2)]
    w_left = [remote(N_W + 2 + h, w_hbm.at[0, parts[h]], wv.at[1, parts[h]], at_x(3)) for h in range(2)]
    wf_right = remote(N_WF, wv.at[3, low], wv.at[2, low], at_x(1))
    wf_left = remote(N_WF + 1, wv.at[1, high], wv.at[2, high], at_x(3))
    gains = [remote(N_GAIN + m - 1, gv.at[0], gv.at[4 - m], at_x(m)) for m in (1, 2, 3)]
    inverse = remote(N_INV, inn.at[0], inn.at[1], pair)
    s2_right = remote(N_S2, s2.at[0], s2r.at[0], at_x(1))
    s2_left = remote(N_S2 + 1, s2.at[1], s2r.at[1], at_x(3))
    s1p_right = remote(N_S1P, s1.at[0, high], s1r.at[0, high], at_x(1))
    s1p_left = remote(N_S1P + 1, s1.at[1, low], s1r.at[1, low], at_x(3))
    s1s_right = remote(N_S1S, s1.at[0, low], s1r.at[0, low], at_x(1))
    s1s_left = remote(N_S1S + 1, s1.at[1, high], s1r.at[1, high], at_x(3))
    inner = remote(N_INNER, ins, inr, pair)
    kv_half = [
        remote(number, kvs.at[pl.ds(p * 128, 128)], kvr.at[pl.ds(p * 128, 128)], pair)
        for p, number in ((0, N_KV), (1, N_KV1))
    ]
    dx_half = [remote(N_DX + j, dxs.at[j], dx_out.at[:, own_cols(j)], pair) for j in range(4)]
    gain_sum = [remote(N_GG + m - 1, gs.at[m], gr.at[m], at_x(m)) for m in (1, 2, 3)]
    frag = [remote(N_FR + k, fr_hbm.at[0, :, y_cols(k)], fr.at[k], core) for k in range(4)]
    y1_right = remote(N_Y1, f2.at[pl.ds(0, 128)], y1r.at[0], at_y(1))
    y1_left = remote(N_Y1 + 1, f2.at[pl.ds(128, 128)], y1r.at[1], at_y(3))
    y2_right = remote(N_Y2, f13.at[0], y2r.at[0], at_y(1))
    y2_left = remote(N_Y2 + 1, f13.at[1], y2r.at[1], at_y(3))
    top, bottom = pl.ds(0, 128), pl.ds(128, 128)
    z1_up = remote(N_Z1, gb.at[2, top], z1r.at[0], at_zh(1))
    z1_down = remote(N_Z1 + 1, gb.at[2, bottom], z1r.at[1], at_zh(3))
    z2_up = remote(N_Z2, gb.at[1], zr.at[0], at_zh(1))
    z2_down = remote(N_Z2 + 1, gb.at[3], zr.at[1], at_zh(3))

    def sy_cols(m):
        return pl.ds(pl.multiple_of(((zh + m) % 4) * 128, 128), 128)

    own_sy = sy.at[0, :, sy_cols(0)]
    zg1_up = remote(N_ZG1, own_sy, own_sy, at_zh(1))
    zg1_down = remote(N_ZG1 + 1, own_sy, own_sy, at_zh(3))
    below, above = sy.at[0, top, sy_cols(3)], sy.at[0, bottom, sy_cols(1)]
    zg2_up = remote(N_ZG2, below, below, at_zh(1))
    zg2_down = remote(N_ZG2 + 1, above, above, at_zh(3))
    g1_right = remote(N_G1, sy.at[0], sy.at[3], at_y(1))
    g1_left = remote(N_G1 + 1, sy.at[0], sy.at[1], at_y(3))
    g2_right = remote(N_G2, sy.at[3, top], sy.at[2, top], at_y(1))
    g2_left = remote(N_G2 + 1, sy.at[1, bottom], sy.at[2, bottom], at_y(3))
    to_core = [remote(N_SY + k, sy.at[k], sp.at[k], core) for k in range(4)]

    load_x = [local(L_X + j, x_hbm.at[:, own_cols(j)], xv.at[j]) for j in range(4)]
    load_x += [local(L_X + 4 + j, x_hbm.at[:, pair_cols(j)], xv.at[4 + j]) for j in range(4)]
    load_c = local(L_C, c_hbm, cv.at[low])
    load_w = local(L_W, w_hbm.at[0], wv.at[0])
    load_fr = [local(L_FR + k, fr_hbm.at[0, :, y_cols(k)], fo.at[k]) for k in range(4)]
    load_op, load_om = local(L_OP, op_hbm, opv), local(L_OM, om_hbm, omv)
    load_idx = local(L_IDX, idx_hbm, idx_ref)
    for copy in load_x + [load_idx, load_c, load_w] + load_fr + [load_op, load_om]:
        copy.start()

    barrier = pltpu.get_barrier_semaphore()
    partners = [pair, core] + [at_x(m) for m in (1, 2, 3)]
    partners += [at_y(1), at_y(3)] + [at_zh(1), at_zh(3)]
    for device in partners:
        pl.semaphore_signal(barrier, inc=1, device_id=device, device_id_type=MESH)
    gv[0] = jnp.broadcast_to(gain_ref[...].astype(F32), (8, BLK))
    pl.semaphore_wait(barrier, len(partners))

    for copy in gains:
        copy.start()
    w_right[0].start()
    w_left[1].start()
    cot.start()
    w_right[1].start()
    w_left[0].start()
    rows[2].start()
    for k in (2, 1, 3, 0):
        frag[k].start()

    def chunks(count, body, carry=0, size=CH):
        def step(i, held):
            return body(pl.ds(pl.multiple_of(i * size, size), size), held)
        return lax.fori_loop(0, count // size, step, carry)

    def statistics(at, held):
        total = jnp.zeros((CH, BLK), F32)
        for j in range(8):
            value = xv[j, at, :].astype(F32)
            total = total + value * value
        mean = jnp.sum(total, axis=1, keepdims=True) * (1.0 / D)
        inv[0, at, :] = jnp.broadcast_to(lax.rsqrt(mean + 1e-05), (CH, 128))
        return held

    def normalise(j, half):
        source = xv if half == 0 else xp

        def step(at, held):
            unit = source[j, at, :].astype(F32) * wide(inv[half, at, :], BLK // 128)
            rows_at = pl.ds(pl.multiple_of(at.start + half * ROWS, CH), CH)
            nv[j, rows_at, :] = (unit * gv[j, 0:1, :]).astype(BF16)
            return held

        chunks(ROWS, step)

    def add_kv(j, first, at=pl.ds(0, 2 * ROWS)):
        def step(t, held):
            cols = pl.ds(pl.multiple_of(t * 256, 256), 256)
            part = jnp.dot(nv[j, at, :], wv[j, :, cols], preferred_element_type=F32)
            if first:
                kacc[at, cols] = part
            else:
                kacc[at, cols] += part
            return held

        lax.fori_loop(0, KV // 256, step, 0)

    def make_hidden(j):
        def step(t, held):
            at = pl.ds(pl.multiple_of(t * 256, 256), 256)
            hv[j, :, at] = lax.dot_general(
                cv[...], wv[j, at, :], (((1,), (1,)), ((), ())), preferred_element_type=F32
            )
            return held

        lax.fori_loop(0, BLK // 256, step, 0)

    def weight_term(j, half, put):
        def step(t, held):
            cols = pl.ds(pl.multiple_of(t * 512, 512), 512)
            put(cols, lax.dot_general(
                nv[j, :, pl.ds(half * 256, 256)], cv[:, cols], (((0,), (0,)), ((), ())),
                preferred_element_type=F32,
            ))
            return held

        lax.fori_loop(0, KV // 512, step, 0)

    def into(ref, *where):
        def put(cols, value):
            ref[(*where, cols)] = value.astype(ref.dtype)
        return put

    def own_part(zz):
        return pl.ds(pl.multiple_of(zz * 256 + c * 128, 128), 128)

    def pair_sum(k, at, zz):
        cols = own_part(zz)
        return fo[k, at, cols].astype(F32) + fr[k, at, cols].astype(F32)

    for copy in load_x:
        copy.wait()
    chunks(ROWS, statistics)
    for half in range(2):
        part = pl.ds(half * 128, 128)
        inn[0, :, part] = jnp.transpose(inv[0, part, :])[0:8, :]
    inverse.start()

    for k in range(4):
        load_fr[k].wait()
    frag[2].wait_recv()

    def sum_f2(at, held):
        for zz in range(4):
            f2[at, pl.ds(zz * 128, 128)] = pair_sum(2, at, zz).astype(BF16)
        return held

    chunks(256, sum_f2)
    y1_right.start()
    y1_left.start()

    for copy in gains:
        copy.wait_recv()
    for j in (2, 1, 3, 0):
        normalise(j, 0)

    y1_right.wait_recv()
    y1_left.wait_recv()

    def sum_f13(side, k, half):
        def plain(at, held):
            there = pl.ds(pl.multiple_of(at.start + (1 - half) * 128, CH), CH)
            for zz in range(4):
                f13[side, there, pl.ds(zz * 128, 128)] = pair_sum(k, there, zz).astype(BF16)
            return held

        def passing(at, held):
            there = pl.ds(pl.multiple_of(at.start + half * 128, CH), CH)
            for zz in range(4):
                cols = pl.ds(zz * 128, 128)
                total = pair_sum(k, there, zz) + y1r[side, at, cols].astype(F32)
                f13[side, there, cols] = total.astype(BF16)
            return held

        frag[k].wait_recv()
        chunks(128, passing)
        chunks(128, plain)

    sum_f13(0, 1, 0)
    y2_right.start()
    sum_f13(1, 3, 1)
    y2_left.start()

    w_right[0].wait_recv()
    wf_right.start()
    w_left[1].wait_recv()
    wf_left.start()

    load_c.wait()
    load_w.wait()
    cot.wait_recv()
    cot.wait_send()
    rows[1].start()
    make_hidden(0)

    frag[0].wait_recv()
    y2_right.wait_recv()
    y2_left.wait_recv()

    def sum_g(m):
        zz = (zh + m) % 4
        cols = pl.ds(pl.multiple_of(zz * 128, 128), 128)

        def step(at, held):
            total = pair_sum(0, at, zz)
            total = total + y2r[0, at, cols].astype(F32) + y2r[1, at, cols].astype(F32)
            if m == 0:
                g0[at, :] = total
            else:
                gb[m, at, :] = total.astype(BF16)
            return held

        chunks(256, step)

    sum_g(2)
    z1_up.start()
    z1_down.start()
    for m in (1, 3, 0):
        sum_g(m)

    inverse.wait_recv()
    for half in range(2):
        part = pl.ds(half * 128, 128)
        inv[1, part, :] = jnp.transpose(jnp.broadcast_to(inn[1, 0:1, part], (128, 128)))
    rows[2].wait_recv()
    rows[2].wait_send()
    rows[3].start()
    normalise(2, 1)
    weight_term(2, 0, into(s2, 0, slice(None)))
    s2_right.start()
    weight_term(2, 1, into(s2, 1, slice(None)))
    s2_left.start()

    def pass_g(side, m, first_row):
        def step(at, held):
            there = pl.ds(pl.multiple_of(at.start + first_row, CH), CH)
            total = gb[m, there, :].astype(F32) + z1r[side, at, :].astype(F32)
            gb[m, there, :] = total.astype(BF16)
            return held

        chunks(128, step)

    z1_up.wait_recv()
    z1_down.wait_recv()
    pass_g(0, 1, 0)
    z2_up.start()
    pass_g(1, 3, 128)
    z2_down.start()

    rows[1].wait_recv()
    rows[1].wait_send()
    rows[0].start()
    normalise(1, 1)
    weight_term(1, 1, into(s1, 0, high))
    s1p_right.start()
    weight_term(1, 0, into(d13, 0, slice(None)))

    rows[3].wait_recv()
    normalise(3, 1)
    weight_term(3, 0, into(s1, 1, low))
    s1p_left.start()
    weight_term(3, 1, into(d13, 1, slice(None)))

    w_right[1].wait_recv()
    w_left[0].wait_recv()
    add_kv(1, True)
    add_kv(3, False)
    wf_right.wait_recv()
    wf_left.wait_recv()
    add_kv(2, False)
    add_kv(0, False, low)

    def inner_step(half):
        def step(at, held):
            there = pl.ds(pl.multiple_of(at.start + half * ROWS, CH), CH)
            product = jnp.zeros((CH, 256), F32)
            for t in range(4):
                cols = pl.ds(t * 256, 256)
                product = product + cv[there, cols].astype(F32) * kacc[there, cols]
            total = jnp.sum(product, axis=1, keepdims=True) * (1.0 / D)
            inv[2 + half, at, :] = jnp.broadcast_to(total, (CH, 128))
            return held

        chunks(ROWS, step)
        for part in range(2):
            there = pl.ds(half * ROWS + part * 128, 128)
            ins[:, there] = jnp.transpose(inv[2 + half, pl.ds(part * 128, 128), :])[0:8, :]

    def round_kv(part):
        def step(at, held):
            there = pl.ds(pl.multiple_of(at.start + part * 128, CH), CH)
            source = pl.ds(pl.multiple_of(at.start + part * 128 + ROWS, CH), CH)
            kvs[there, :] = kacc[source, :].astype(BF16)
            return held

        chunks(128, step)

    z2_up.wait_recv()
    z2_down.wait_recv()
    load_op.wait()
    load_om.wait()
    load_idx.wait()
    chosen = idx_ref[0]

    def update(at, held):
        total = g0[at, :] + zr[0, at, :].astype(F32) + zr[1, at, :].astype(F32)
        now = opv[chosen, at, :]
        pseudo = now - total * (1.0 / 32.0)
        moment = 0.9 * omv[chosen, at, :] + pseudo
        new = now - 0.7 * (pseudo + 0.9 * moment)
        nm_out[at, :] = moment
        np_out[at, :] = new
        sy[0, at, sy_cols(0)] = new.astype(BF16)
        return held

    chunks(256, update)

    inner_step(0)
    rows[0].wait_recv()
    zg1_up.start()
    zg1_down.start()
    normalise(0, 1)
    add_kv(0, False, high)
    round_kv(0)
    kv_half[0].start()
    inner_step(1)
    inner.start()
    round_kv(1)
    kv_half[1].start()
    zg1_up.wait_recv()
    zg2_up.start()
    zg1_down.wait_recv()
    zg2_down.start()
    make_hidden(1)
    make_hidden(3)
    make_hidden(2)

    def add_passing(side, first_row):
        def step(at, held):
            there = pl.ds(pl.multiple_of(at.start + first_row, CH), CH)
            s1[side, there, :] = (d13[side, at, :] + s2r[side, at, :].astype(F32)).astype(BF16)
            return held
        chunks(256, step)

    s2_right.wait_recv()
    add_passing(0, 0)
    s1s_right.start()
    s2_left.wait_recv()
    add_passing(1, 256)
    s1s_left.start()

    zg2_up.wait_recv()
    zg2_down.wait_recv()
    g1_right.start()
    g1_left.start()
    to_core[0].start()

    inner.wait_recv()
    for half in range(2):
        for part in range(2):
            mine = pl.ds(half * ROWS + part * 128, 128)
            theirs = pl.ds((1 - half) * ROWS + part * 128, 128)
            total = ins[0:1, mine] + inr[0:1, theirs]
            inv[2 + half, pl.ds(part * 128, 128), :] = jnp.transpose(
                jnp.broadcast_to(total, (128, 128))
            )

    def input_grad(j, half, put):
        source = xv if half == 0 else xp

        def step(at, held):
            there = pl.ds(pl.multiple_of(at.start + half * ROWS, CH), CH)
            scale = wide(inv[half, at, :], BLK // 128)
            unit = source[j, at, :].astype(F32) * scale
            hidden = hv[j, there, :]
            term = (hidden * unit).reshape(CH // 8, 8, BLK)
            scaled = hidden * gv[j, 0:1, :]
            mean = wide(inv[2 + half, at, :], BLK // 128)
            put(at, (scale * (scaled - unit * mean)).astype(BF16))
            return held + jnp.sum(term, axis=0)

        return chunks(ROWS, step, jnp.zeros((8, BLK), F32))

    def put_pair(j):
        def put(at, value):
            dxs[j, at, :] = value
        return put

    def put_own(j):
        def put(at, value):
            dx_out[at, own_cols(j)] = value
        return put

    for j in range(4):
        gs[j] = input_grad(j, 1, put_pair(j))
        dx_half[j].start()

    for j in (1, 2, 3, 0):
        total = gs[j] + input_grad(j, 0, put_own(j))
        gs[j] = jnp.broadcast_to(jnp.sum(total, axis=0, keepdims=True), (8, BLK))
        if j > 0:
            gain_sum[j - 1].start()

    g1_right.wait_recv()
    g2_right.start()
    g1_left.wait_recv()
    g2_left.start()
    to_core[3].start()
    to_core[1].start()

    weight_term(0, 0, into(d0, low))
    weight_term(0, 1, into(d0, high))

    def place(k):
        to_core[k].wait_recv()
        first = ((y + k) % 4) * 1024

        def step(at, held):
            for zz in range(4):
                cols = pl.ds(zz * 128, 128)
                mine = pl.ds(pl.multiple_of(first + zz * 256 + c * 128, 128), 128)
                theirs = pl.ds(pl.multiple_of(first + zz * 256 + (1 - c) * 128, 128), 128)
                sy_out[at, mine] = sy[k, at, cols]
                sy_out[at, theirs] = sp[k, at, cols]
            return held

        chunks(256, step)

    place(0)
    g2_right.wait_recv()
    g2_left.wait_recv()
    to_core[2].start()
    place(3)
    place(1)

    for copy in kv_half:
        copy.wait_recv()

    def finish_kv(at, held):
        kv_out[at, :] = (kacc[at, :] + kvr[at, :].astype(F32)).astype(BF16)
        return held

    chunks(ROWS, finish_kv)
    place(2)
    for copy in gain_sum:
        copy.wait_recv()
    dg_out[...] = gs[0] + gr[1] + gr[2] + gr[3]
    for copy in (s1p_right, s1p_left, s1s_right, s1s_left):
        copy.wait_recv()

    def finish_dw(at, held):
        total = d0[at, :] + s1r[0, at, :].astype(F32) + s1r[1, at, :].astype(F32)
        dw_out[at, :] = total.astype(BF16)
        return held

    chunks(BLK, finish_dw)
    for copy in dx_half:
        copy.wait_recv()

    for copy in (
        w_right + w_left + [rows[3], rows[0], wf_right, wf_left, inverse, s2_right, s2_left]
        + [s1p_right, s1p_left, s1s_right, s1s_left, inner]
        + kv_half
        + [y1_right, y1_left, y2_right, y2_left, g1_right, g1_left, g2_right, g2_left]
        + gains + dx_half + gain_sum + frag + [zg1_up, zg1_down, zg2_up, zg2_down] + [z1_up, z1_down, z2_up, z2_down] + to_core
    ):
        copy.wait_send()


def store(kv, dx, dw, dg, np_, nm, sy, kv_out, dx_out, dw_out, dg_out, np_out, nm_out, sy_out, sem):
    copies = [
        pltpu.make_async_copy(source, target, sem.at[i])
        for i, (source, target) in enumerate(
            ((dx, dx_out), (sy, sy_out), (dw, dw_out.at[0]), (kv, kv_out), (np_, np_out), (nm, nm_out))
        )
    ]
    for copy in copies:
        copy.start()
    dg_out[...] = dg[0:1, :].astype(BF16)
    for copy in copies:
        copy.wait()


def on_device(x, gain, w, cot, frag, params, moment, index):
    any_spec = pl.BlockSpec(memory_space=pl.ANY)
    vmem = pl.BlockSpec(memory_space=pltpu.VMEM)
    out = jax.ShapeDtypeStruct
    held = pl.pallas_call(
        kernel,
        out_shape=(
            pltpu.VMEM((ROWS, KV), BF16), pltpu.VMEM((ROWS, D), BF16), pltpu.VMEM((BLK, KV), BF16),
            pltpu.VMEM((8, BLK), F32), pltpu.VMEM((256, 128), F32), pltpu.VMEM((256, 128), F32),
            pltpu.VMEM((256, D), BF16),
        ),
        in_specs=[any_spec, vmem] + [any_spec] * 6,
        out_specs=(vmem,) * 7,
        scratch_shapes=[
            pltpu.VMEM((8, ROWS, BLK), BF16),
            pltpu.VMEM((4, ROWS, BLK), BF16),
            pltpu.VMEM((2 * ROWS, KV), BF16),
            pltpu.VMEM((4, BLK, KV), BF16),
            pltpu.VMEM((4, 8, BLK), F32),
            pltpu.VMEM((4, ROWS, 128), F32),
            pltpu.VMEM((4, 2 * ROWS, BLK), BF16),
            pltpu.VMEM((4, 2 * ROWS, BLK), F32),
            pltpu.VMEM((2 * ROWS, KV), F32),
            pltpu.VMEM((BLK, KV), F32),
            pltpu.VMEM((2, 256, KV), F32),
            pltpu.VMEM((2, 256, KV), BF16),
            pltpu.VMEM((2, 256, KV), BF16),
            pltpu.VMEM((2, BLK, KV), BF16),
            pltpu.VMEM((2, BLK, KV), BF16),
            pltpu.VMEM((2, 8, ROWS), F32),
            pltpu.VMEM((8, 2 * ROWS), F32),
            pltpu.VMEM((8, 2 * ROWS), F32),
            pltpu.VMEM((ROWS, KV), BF16),
            pltpu.VMEM((ROWS, KV), BF16),
            pltpu.VMEM((4, ROWS, BLK), BF16),
            pltpu.VMEM((4, 8, BLK), F32),
            pltpu.VMEM((4, 8, BLK), F32),
            pltpu.VMEM((4, 256, 1024), BF16),
            pltpu.VMEM((4, 256, 1024), BF16),
            pltpu.VMEM((256, 512), BF16),
            pltpu.VMEM((2, 128, 512), BF16),
            pltpu.VMEM((2, 256, 512), BF16),
            pltpu.VMEM((2, 256, 512), BF16),
            pltpu.VMEM((4, 256, 128), BF16),
            pltpu.VMEM((256, 128), F32),
            pltpu.VMEM((2, 128, 128), BF16),
            pltpu.VMEM((2, 256, 128), BF16),
            pltpu.VMEM((4, 256, 128), F32),
            pltpu.VMEM((4, 256, 128), F32),
            pltpu.VMEM((4, 256, 512), BF16),
            pltpu.VMEM((4, 256, 512), BF16),
            pltpu.SMEM((1,), jnp.int32),
            pltpu.SemaphoreType.DMA((N_REMOTE,)),
            pltpu.SemaphoreType.DMA((N_REMOTE,)),
            pltpu.SemaphoreType.DMA((N_LOCAL,)),
        ],
        compiler_params=pltpu.CompilerParams(
            collective_id=0, has_side_effects=True, vmem_limit_bytes=52 * 1024 * 1024
        ),
        cost_estimate=pl.CostEstimate(
            flops=6 * ROWS * D * KV, bytes_accessed=24 << 20, transcendentals=ROWS
        ),
    )(x, gain, w, cot, frag, params, moment, index)
    return pl.pallas_call(
        store,
        out_shape=(
            out((ROWS, KV), BF16), out((ROWS, D), BF16), out((1, BLK, KV), BF16),
            out((1, BLK), BF16), out((256, 128), F32), out((256, 128), F32),
            out((256, D), BF16),
        ),
        in_specs=[vmem] * 7,
        out_specs=(any_spec, any_spec, any_spec, vmem, any_spec, any_spec, any_spec),
        scratch_shapes=[pltpu.SemaphoreType.DMA((6,))],
        compiler_params=pltpu.CompilerParams(vmem_limit_bytes=2 * 1024 * 1024),
    )(*held)


def solution(mesh):
    return jax.shard_map(
        on_device,
        mesh=mesh,
        in_specs=(
            P(("rep", "fsdp"), None),
            P("rep", "fsdp"),
            P("rep", "fsdp", None),
            P(("rep", "fsdp"), None),
            P("rep", "fsdp", None),
            P(None, "fsdp", "rep"),
            P(None, "fsdp", "rep"),
            P(),
        ),
        out_specs=(
            P(("rep", "fsdp"), None),
            P(("rep", "fsdp"), None),
            P("rep", "fsdp", None),
            P("rep", "fsdp"),
            P("fsdp", "rep"),
            P("fsdp", "rep"),
            P("fsdp", None),
        ),
        check_vma=False,
    )
```

```python
import jax
import jax.numpy as jnp
from jax import lax
from jax.experimental import pallas as pl
from jax.experimental.pallas import tpu as pltpu
from jax.sharding import PartitionSpec as P

MESH = pl.DeviceIdType.MESH
F32, BF16 = jnp.float32, jnp.bfloat16
D = 4096
ROWS = 256
BLK = 512
KV = 1024
CH = 32

N_COT, N_X, N_W, N_GAIN, N_INV = 0, 1, 5, 9, 12
N_WF, N_KV1, N_Z2, N_ZG2 = 50, 52, 53, 55
N_COT1, N_S2B, N_S1PB, N_S1SB = 57, 58, 60, 62
N_S2, N_S1P, N_S1S, N_INNER, N_KV, N_DX, N_GG = 13, 15, 17, 19, 20, 21, 25
N_FR, N_Y1, N_Y2, N_Z1, N_ZG1, N_G1, N_G2, N_SY = 28, 32, 34, 36, 39, 42, 44, 46
N_REMOTE = 64
L_X, L_C, L_W, L_FR, L_OP, L_OM, L_IDX = 0, 8, 9, 10, 14, 15, 16
N_LOCAL = 17


def wide(value, times):
    return jnp.concatenate([value] * times, axis=1)


def kernel(
    x_hbm, gain_ref, w_hbm, c_hbm, fr_hbm, op_hbm, om_hbm, idx_hbm,
    kv_out, dx_out, dw_out, dg_out, np_out, nm_out, sy_out,
    xv, xp, cv, wv, gv, inv, nv, hv, kacc, d0, d13, s2, s2r, s1, s1r,
    inn, ins, inr, kvs, kvr, dxs, gs, gr,
    fo, fr, f2, y1r, f13, y2r, gb, g0, z1r, zr, opv, omv, sy, sp, idx_ref,
    ssem, rsem, lsem,
):
    f, r = lax.axis_index("fsdp"), lax.axis_index("rep")
    x, z = f // 2, f % 2
    y, zh, c = r // 8, (r // 2) % 4, r % 2

    def at_x(step):
        return {"fsdp": ((x + step) % 4) * 2 + z}

    def at_y(step):
        return {"rep": ((y + step) % 4) * 8 + zh * 2 + c}

    def at_zh(step):
        return {"rep": y * 8 + ((zh + step) % 4) * 2 + c}

    pair, core = {"fsdp": x * 2 + 1 - z}, {"rep": y * 8 + zh * 2 + 1 - c}

    def remote(number, source, target, device):
        return pltpu.make_async_remote_copy(
            src_ref=source, dst_ref=target, send_sem=ssem.at[number], recv_sem=rsem.at[number],
            device_id=device, device_id_type=MESH,
        )

    def local(number, source, target):
        return pltpu.make_async_copy(source, target, lsem.at[number])

    def own_cols(j):
        return pl.ds(pl.multiple_of((((x + j) % 4) * 2 + z) * BLK, BLK), BLK)

    def pair_cols(j):
        return pl.ds(pl.multiple_of((((x + j) % 4) * 2 + 1 - z) * BLK, BLK), BLK)

    def y_cols(k):
        return pl.ds(pl.multiple_of(((y + k) % 4) * 1024, 1024), 1024)

    low, high = pl.ds(0, ROWS), pl.ds(ROWS, ROWS)

    cols = (pl.ds(0, 512), pl.ds(512, 512))
    cot = [
        remote(number, c_hbm.at[:, cols[t]], cv.at[high, cols[t]], pair)
        for t, number in ((0, N_COT), (1, N_COT1))
    ]
    rows = [remote(N_X + j, x_hbm.at[:, pair_cols(j)], xp.at[j], pair) for j in range(4)]
    parts = (low, high)
    w_right = [remote(N_W + h, w_hbm.at[0, parts[h]], wv.at[3, parts[h]], at_x(1)) for h in range(2)]
    w_left = [remote(N_W + 2 + h, w_hbm.at[0, parts[h]], wv.at[1, parts[h]], at_x(3)) for h in range(2)]
    wf_right = remote(N_WF, wv.at[3, low], wv.at[2, low], at_x(1))
    wf_left = remote(N_WF + 1, wv.at[1, high], wv.at[2, high], at_x(3))
    gains = [remote(N_GAIN + m - 1, gv.at[0], gv.at[4 - m], at_x(m)) for m in (1, 2, 3)]
    inverse = remote(N_INV, inn.at[0], inn.at[1], pair)
    s2_right = [remote(n, s2.at[0, :, cols[t]], s2r.at[0, :, cols[t]], at_x(1)) for t, n in ((0, N_S2), (1, N_S2B))]
    s2_left = [remote(n + 1, s2.at[1, :, cols[t]], s2r.at[1, :, cols[t]], at_x(3)) for t, n in ((0, N_S2), (1, N_S2B))]
    s1p_right = [remote(n, s1.at[0, high, cols[t]], s1r.at[0, high, cols[t]], at_x(1)) for t, n in ((0, N_S1P), (1, N_S1PB))]
    s1p_left = [remote(n + 1, s1.at[1, low, cols[t]], s1r.at[1, low, cols[t]], at_x(3)) for t, n in ((0, N_S1P), (1, N_S1PB))]
    s1s_right = [remote(n, s1.at[0, low, cols[t]], s1r.at[0, low, cols[t]], at_x(1)) for t, n in ((0, N_S1S), (1, N_S1SB))]
    s1s_left = [remote(n + 1, s1.at[1, high, cols[t]], s1r.at[1, high, cols[t]], at_x(3)) for t, n in ((0, N_S1S), (1, N_S1SB))]
    inner = remote(N_INNER, ins, inr, pair)
    kv_half = [
        remote(number, kvs.at[pl.ds(p * 128, 128)], kvr.at[pl.ds(p * 128, 128)], pair)
        for p, number in ((0, N_KV), (1, N_KV1))
    ]
    dx_half = [remote(N_DX + j, dxs.at[j], dx_out.at[:, own_cols(j)], pair) for j in range(4)]
    gain_sum = [remote(N_GG + m - 1, gs.at[m], gr.at[m], at_x(m)) for m in (1, 2, 3)]
    frag = [remote(N_FR + k, fr_hbm.at[0, :, y_cols(k)], fr.at[k], core) for k in range(4)]
    y1_right = remote(N_Y1, f2.at[pl.ds(0, 128)], y1r.at[0], at_y(1))
    y1_left = remote(N_Y1 + 1, f2.at[pl.ds(128, 128)], y1r.at[1], at_y(3))
    y2_right = remote(N_Y2, f13.at[0], y2r.at[0], at_y(1))
    y2_left = remote(N_Y2 + 1, f13.at[1], y2r.at[1], at_y(3))
    top, bottom = pl.ds(0, 128), pl.ds(128, 128)
    z1_up = remote(N_Z1, gb.at[2, top], z1r.at[0], at_zh(1))
    z1_down = remote(N_Z1 + 1, gb.at[2, bottom], z1r.at[1], at_zh(3))
    z2_up = remote(N_Z2, gb.at[1], zr.at[0], at_zh(1))
    z2_down = remote(N_Z2 + 1, gb.at[3], zr.at[1], at_zh(3))

    def sy_cols(m):
        return pl.ds(pl.multiple_of(((zh + m) % 4) * 128, 128), 128)

    own_sy = sy.at[0, :, sy_cols(0)]
    zg1_up = remote(N_ZG1, own_sy, own_sy, at_zh(1))
    zg1_down = remote(N_ZG1 + 1, own_sy, own_sy, at_zh(3))
    below, above = sy.at[0, top, sy_cols(3)], sy.at[0, bottom, sy_cols(1)]
    zg2_up = remote(N_ZG2, below, below, at_zh(1))
    zg2_down = remote(N_ZG2 + 1, above, above, at_zh(3))
    g1_right = remote(N_G1, sy.at[0], sy.at[3], at_y(1))
    g1_left = remote(N_G1 + 1, sy.at[0], sy.at[1], at_y(3))
    g2_right = remote(N_G2, sy.at[3, top], sy.at[2, top], at_y(1))
    g2_left = remote(N_G2 + 1, sy.at[1, bottom], sy.at[2, bottom], at_y(3))
    to_core = [remote(N_SY + k, sy.at[k], sp.at[k], core) for k in range(4)]

    barrier = pltpu.get_barrier_semaphore()
    partners = [pair, core] + [at_x(m) for m in (1, 2, 3)]
    partners += [at_y(1), at_y(3)] + [at_zh(1), at_zh(3)]
    for device in partners:
        pl.semaphore_signal(barrier, inc=1, device_id=device, device_id_type=MESH)
    load_x = [local(L_X + j, x_hbm.at[:, own_cols(j)], xv.at[j]) for j in range(4)]
    load_x += [local(L_X + 4 + j, x_hbm.at[:, pair_cols(j)], xv.at[4 + j]) for j in range(4)]
    load_c = local(L_C, c_hbm, cv.at[low])
    load_w = local(L_W, w_hbm.at[0], wv.at[0])
    load_fr = [local(L_FR + k, fr_hbm.at[0, :, y_cols(k)], fo.at[k]) for k in range(4)]
    load_op, load_om = local(L_OP, op_hbm, opv), local(L_OM, om_hbm, omv)
    load_idx = local(L_IDX, idx_hbm, idx_ref)
    for copy in load_x + [load_idx, load_c, load_w] + load_fr + [load_op, load_om]:
        copy.start()

    gv[0] = jnp.broadcast_to(gain_ref[...].astype(F32), (8, BLK))
    pl.semaphore_wait(barrier, len(partners))

    w_right[0].start()
    rows[2].start()
    w_left[1].start()
    frag[2].start()
    cot[0].start()
    for copy in gains:
        copy.start()
    w_right[1].start()
    w_left[0].start()
    rows[1].start()
    for k in (1, 3, 0):
        frag[k].start()

    def chunks(count, body, carry=0, size=CH):
        def step(i, held):
            return body(pl.ds(pl.multiple_of(i * size, size), size), held)
        return lax.fori_loop(0, count // size, step, carry)

    def statistics(at, held):
        total = jnp.zeros((CH, BLK), F32)
        for j in range(8):
            value = xv[j, at, :].astype(F32)
            total = total + value * value
        mean = jnp.sum(total, axis=1, keepdims=True) * (1.0 / D)
        inv[0, at, :] = jnp.broadcast_to(lax.rsqrt(mean + 1e-05), (CH, 128))
        return held

    def normalise(j, half):
        source = xv if half == 0 else xp

        def step(at, held):
            unit = source[j, at, :].astype(F32) * wide(inv[half, at, :], BLK // 128)
            rows_at = pl.ds(pl.multiple_of(at.start + half * ROWS, CH), CH)
            nv[j, rows_at, :] = (unit * gv[j, 0:1, :]).astype(BF16)
            return held

        chunks(ROWS, step)

    def add_kv(j, first, at=pl.ds(0, 2 * ROWS)):
        def step(t, held):
            cols = pl.ds(pl.multiple_of(t * 256, 256), 256)
            part = jnp.dot(nv[j, at, :], wv[j, :, cols], preferred_element_type=F32)
            if first:
                kacc[at, cols] = part
            else:
                kacc[at, cols] += part
            return held

        lax.fori_loop(0, KV // 256, step, 0)

    def make_hidden(j):
        def step(t, held):
            at = pl.ds(pl.multiple_of(t * 256, 256), 256)
            hv[j, :, at] = lax.dot_general(
                cv[...], wv[j, at, :], (((1,), (1,)), ((), ())), preferred_element_type=F32
            )
            return held

        lax.fori_loop(0, BLK // 256, step, 0)

    def weight_term(j, half, t, put):
        put(cols[t], lax.dot_general(
            nv[j, :, pl.ds(half * 256, 256)], cv[:, cols[t]], (((0,), (0,)), ((), ())),
            preferred_element_type=F32,
        ))

    def into(ref, *where):
        def put(cols, value):
            ref[(*where, cols)] = value.astype(ref.dtype)
        return put

    def own_part(zz):
        return pl.ds(pl.multiple_of(zz * 256 + c * 128, 128), 128)

    def pair_sum(k, at, zz):
        cols = own_part(zz)
        return fo[k, at, cols].astype(F32) + fr[k, at, cols].astype(F32)

    for copy in load_x:
        copy.wait()
    chunks(ROWS, statistics)
    for half in range(2):
        part = pl.ds(half * 128, 128)
        inn[0, :, part] = jnp.transpose(inv[0, part, :])[0:8, :]
    inverse.start()

    for k in range(4):
        load_fr[k].wait()
    frag[2].wait_recv()

    def sum_f2(at, held):
        for zz in range(4):
            f2[at, pl.ds(zz * 128, 128)] = pair_sum(2, at, zz).astype(BF16)
        return held

    chunks(256, sum_f2)
    y1_right.start()
    y1_left.start()

    for copy in gains:
        copy.wait_recv()
    for j in (2, 1, 3, 0):
        normalise(j, 0)

    y1_right.wait_recv()
    y1_left.wait_recv()

    def sum_f13(side, k, half):
        def plain(at, held):
            there = pl.ds(pl.multiple_of(at.start + (1 - half) * 128, CH), CH)
            for zz in range(4):
                f13[side, there, pl.ds(zz * 128, 128)] = pair_sum(k, there, zz).astype(BF16)
            return held

        def passing(at, held):
            there = pl.ds(pl.multiple_of(at.start + half * 128, CH), CH)
            for zz in range(4):
                cols = pl.ds(zz * 128, 128)
                total = pair_sum(k, there, zz) + y1r[side, at, cols].astype(F32)
                f13[side, there, cols] = total.astype(BF16)
            return held

        frag[k].wait_recv()
        chunks(128, passing)
        chunks(128, plain)

    sum_f13(0, 1, 0)
    y2_right.start()
    sum_f13(1, 3, 1)
    y2_left.start()

    w_right[0].wait_recv()
    wf_right.start()
    w_left[1].wait_recv()
    wf_left.start()

    load_c.wait()
    load_w.wait()
    rows[2].wait_send()
    rows[3].start()

    frag[0].wait_recv()
    y2_right.wait_recv()
    y2_left.wait_recv()

    def sum_g(m):
        zz = (zh + m) % 4
        cols = pl.ds(pl.multiple_of(zz * 128, 128), 128)

        def step(at, held):
            total = pair_sum(0, at, zz)
            total = total + y2r[0, at, cols].astype(F32) + y2r[1, at, cols].astype(F32)
            if m == 0:
                g0[at, :] = total
            else:
                gb[m, at, :] = total.astype(BF16)
            return held

        chunks(256, step)

    sum_g(2)
    z1_up.start()
    z1_down.start()
    for m in (1, 3, 0):
        sum_g(m)

    inverse.wait_recv()
    for half in range(2):
        part = pl.ds(half * 128, 128)
        inv[1, part, :] = jnp.transpose(jnp.broadcast_to(inn[1, 0:1, part], (128, 128)))
    rows[2].wait_recv()
    rows[0].start()
    normalise(2, 1)
    cot[0].wait_recv()
    weight_term(2, 0, 0, into(s2, 0, slice(None)))
    s2_right[0].start()
    weight_term(2, 1, 0, into(s2, 1, slice(None)))
    s2_left[0].start()

    def pass_g(side, m, first_row):
        def step(at, held):
            there = pl.ds(pl.multiple_of(at.start + first_row, CH), CH)
            total = gb[m, there, :].astype(F32) + z1r[side, at, :].astype(F32)
            gb[m, there, :] = total.astype(BF16)
            return held

        chunks(128, step)

    z1_up.wait_recv()
    z1_down.wait_recv()
    pass_g(0, 1, 0)
    z2_up.start()
    pass_g(1, 3, 128)
    z2_down.start()

    rows[1].wait_recv()
    rows[1].wait_send()
    cot[1].start()
    normalise(1, 1)
    weight_term(1, 1, 0, into(s1, 0, high))
    s1p_right[0].start()
    weight_term(1, 0, 0, into(d13, 0, slice(None)))
    rows[3].wait_recv()
    normalise(3, 1)
    weight_term(3, 0, 0, into(s1, 1, low))
    s1p_left[0].start()
    weight_term(3, 1, 0, into(d13, 1, slice(None)))

    w_right[1].wait_recv()
    w_left[0].wait_recv()
    add_kv(1, True)
    add_kv(3, False)
    wf_right.wait_recv()
    wf_left.wait_recv()
    add_kv(2, False)
    add_kv(0, False, low)

    def inner_step(half):
        def step(at, held):
            there = pl.ds(pl.multiple_of(at.start + half * ROWS, CH), CH)
            product = jnp.zeros((CH, 256), F32)
            for t in range(4):
                cols = pl.ds(t * 256, 256)
                product = product + cv[there, cols].astype(F32) * kacc[there, cols]
            total = jnp.sum(product, axis=1, keepdims=True) * (1.0 / D)
            inv[2 + half, at, :] = jnp.broadcast_to(total, (CH, 128))
            return held

        chunks(ROWS, step)
        for part in range(2):
            there = pl.ds(half * ROWS + part * 128, 128)
            ins[:, there] = jnp.transpose(inv[2 + half, pl.ds(part * 128, 128), :])[0:8, :]

    def round_kv(part):
        def step(at, held):
            there = pl.ds(pl.multiple_of(at.start + part * 128, CH), CH)
            source = pl.ds(pl.multiple_of(at.start + part * 128 + ROWS, CH), CH)
            kvs[there, :] = kacc[source, :].astype(BF16)
            return held

        chunks(128, step)

    z2_up.wait_recv()
    z2_down.wait_recv()
    load_op.wait()
    load_om.wait()
    load_idx.wait()
    chosen = idx_ref[0]

    def update(at, held):
        total = g0[at, :] + zr[0, at, :].astype(F32) + zr[1, at, :].astype(F32)
        now = opv[chosen, at, :]
        pseudo = now - total * (1.0 / 32.0)
        moment = 0.9 * omv[chosen, at, :] + pseudo
        new = now - 0.7 * (pseudo + 0.9 * moment)
        nm_out[at, :] = moment
        np_out[at, :] = new
        sy[0, at, sy_cols(0)] = new.astype(BF16)
        return held

    chunks(256, update)

    inner_step(0)
    rows[0].wait_recv()
    zg1_up.start()
    zg1_down.start()
    normalise(0, 1)
    add_kv(0, False, high)
    round_kv(0)
    kv_half[0].start()
    round_kv(1)

    cot[1].wait_recv()
    inner_step(1)
    inner.start()
    kv_half[1].start()
    weight_term(2, 0, 1, into(s2, 0, slice(None)))
    s2_right[1].start()
    weight_term(2, 1, 1, into(s2, 1, slice(None)))
    s2_left[1].start()
    zg1_up.wait_recv()
    zg2_up.start()
    zg1_down.wait_recv()
    zg2_down.start()
    weight_term(1, 1, 1, into(s1, 0, high))
    s1p_right[1].start()
    weight_term(3, 0, 1, into(s1, 1, low))
    s1p_left[1].start()
    weight_term(1, 0, 1, into(d13, 0, slice(None)))
    weight_term(3, 1, 1, into(d13, 1, slice(None)))
    for j in range(4):
        make_hidden(j)

    def add_passing(side, first_row, t):
        def step(at, held):
            there = pl.ds(pl.multiple_of(at.start + first_row, CH), CH)
            total = d13[side, at, cols[t]] + s2r[side, at, cols[t]].astype(F32)
            s1[side, there, cols[t]] = total.astype(BF16)
            return held
        chunks(256, step)

    def pass_on(t):
        s2_right[t].wait_recv()
        add_passing(0, 0, t)
        s1s_right[t].start()
        s2_left[t].wait_recv()
        add_passing(1, 256, t)
        s1s_left[t].start()

    pass_on(0)

    inner.wait_recv()
    for half in range(2):
        for part in range(2):
            mine = pl.ds(half * ROWS + part * 128, 128)
            theirs = pl.ds((1 - half) * ROWS + part * 128, 128)
            total = ins[0:1, mine] + inr[0:1, theirs]
            inv[2 + half, pl.ds(part * 128, 128), :] = jnp.transpose(
                jnp.broadcast_to(total, (128, 128))
            )

    def input_grad(j, half, put):
        source = xv if half == 0 else xp

        def step(at, held):
            there = pl.ds(pl.multiple_of(at.start + half * ROWS, CH), CH)
            scale = wide(inv[half, at, :], BLK // 128)
            unit = source[j, at, :].astype(F32) * scale
            hidden = hv[j, there, :]
            term = (hidden * unit).reshape(CH // 8, 8, BLK)
            scaled = hidden * gv[j, 0:1, :]
            mean = wide(inv[2 + half, at, :], BLK // 128)
            put(at, (scale * (scaled - unit * mean)).astype(BF16))
            return held + jnp.sum(term, axis=0)

        return chunks(ROWS, step, jnp.zeros((8, BLK), F32))

    def put_pair(j):
        def put(at, value):
            dxs[j, at, :] = value
        return put

    def put_own(j):
        def put(at, value):
            dx_out[at, own_cols(j)] = value
        return put

    for j in range(4):
        gs[j] = input_grad(j, 1, put_pair(j))
        dx_half[j].start()

    pass_on(1)

    zg2_up.wait_recv()
    zg2_down.wait_recv()
    g1_right.start()
    g1_left.start()
    to_core[0].start()

    for j in (1, 2, 3, 0):
        total = gs[j] + input_grad(j, 0, put_own(j))
        gs[j] = jnp.broadcast_to(jnp.sum(total, axis=0, keepdims=True), (8, BLK))
        if j > 0:
            gain_sum[j - 1].start()

    g1_right.wait_recv()
    g2_right.start()
    g1_left.wait_recv()
    g2_left.start()
    to_core[3].start()
    to_core[1].start()

    for t in range(2):
        weight_term(0, 0, t, into(d0, low))
        weight_term(0, 1, t, into(d0, high))

    def place(k):
        to_core[k].wait_recv()
        first = ((y + k) % 4) * 1024

        def step(at, held):
            for zz in range(4):
                cols = pl.ds(zz * 128, 128)
                mine = pl.ds(pl.multiple_of(first + zz * 256 + c * 128, 128), 128)
                theirs = pl.ds(pl.multiple_of(first + zz * 256 + (1 - c) * 128, 128), 128)
                sy_out[at, mine] = sy[k, at, cols]
                sy_out[at, theirs] = sp[k, at, cols]
            return held

        chunks(256, step)

    place(0)
    g2_right.wait_recv()
    g2_left.wait_recv()
    to_core[2].start()
    place(3)
    place(1)

    for copy in kv_half:
        copy.wait_recv()

    def finish_kv(at, held):
        kv_out[at, :] = (kacc[at, :] + kvr[at, :].astype(F32)).astype(BF16)
        return held

    chunks(ROWS, finish_kv)
    place(2)
    for copy in gain_sum:
        copy.wait_recv()
    dg_out[...] = gs[0] + gr[1] + gr[2] + gr[3]
    for copy in s1p_right + s1p_left + s1s_right + s1s_left:
        copy.wait_recv()

    def finish_dw(at, held):
        total = d0[at, :] + s1r[0, at, :].astype(F32) + s1r[1, at, :].astype(F32)
        dw_out[at, :] = total.astype(BF16)
        return held

    chunks(BLK, finish_dw)
    for copy in dx_half:
        copy.wait_recv()

    for copy in (
        w_right + w_left + cot + [rows[3], rows[0], wf_right, wf_left, inverse, inner]
        + s2_right + s2_left + s1p_right + s1p_left + s1s_right + s1s_left
        + kv_half
        + [y1_right, y1_left, y2_right, y2_left, g1_right, g1_left, g2_right, g2_left]
        + gains + dx_half + gain_sum + frag + [zg1_up, zg1_down, zg2_up, zg2_down] + [z1_up, z1_down, z2_up, z2_down] + to_core
    ):
        copy.wait_send()


def store(kv, dx, dw, dg, np_, nm, sy, kv_out, dx_out, dw_out, dg_out, np_out, nm_out, sy_out, sem):
    copies = [
        pltpu.make_async_copy(source, target, sem.at[i])
        for i, (source, target) in enumerate(
            ((dx, dx_out), (sy, sy_out), (dw, dw_out.at[0]), (kv, kv_out), (np_, np_out), (nm, nm_out))
        )
    ]
    for copy in copies:
        copy.start()
    dg_out[...] = dg[0:1, :].astype(BF16)
    for copy in copies:
        copy.wait()


def on_device(x, gain, w, cot, frag, params, moment, index):
    any_spec = pl.BlockSpec(memory_space=pl.ANY)
    vmem = pl.BlockSpec(memory_space=pltpu.VMEM)
    out = jax.ShapeDtypeStruct
    held = pl.pallas_call(
        kernel,
        out_shape=(
            pltpu.VMEM((ROWS, KV), BF16), pltpu.VMEM((ROWS, D), BF16), pltpu.VMEM((BLK, KV), BF16),
            pltpu.VMEM((8, BLK), F32), pltpu.VMEM((256, 128), F32), pltpu.VMEM((256, 128), F32),
            pltpu.VMEM((256, D), BF16),
        ),
        in_specs=[any_spec, vmem] + [any_spec] * 6,
        out_specs=(vmem,) * 7,
        scratch_shapes=[
            pltpu.VMEM((8, ROWS, BLK), BF16),
            pltpu.VMEM((4, ROWS, BLK), BF16),
            pltpu.VMEM((2 * ROWS, KV), BF16),
            pltpu.VMEM((4, BLK, KV), BF16),
            pltpu.VMEM((4, 8, BLK), F32),
            pltpu.VMEM((4, ROWS, 128), F32),
            pltpu.VMEM((4, 2 * ROWS, BLK), BF16),
            pltpu.VMEM((4, 2 * ROWS, BLK), F32),
            pltpu.VMEM((2 * ROWS, KV), F32),
            pltpu.VMEM((BLK, KV), F32),
            pltpu.VMEM((2, 256, KV), F32),
            pltpu.VMEM((2, 256, KV), BF16),
            pltpu.VMEM((2, 256, KV), BF16),
            pltpu.VMEM((2, BLK, KV), BF16),
            pltpu.VMEM((2, BLK, KV), BF16),
            pltpu.VMEM((2, 8, ROWS), F32),
            pltpu.VMEM((8, 2 * ROWS), F32),
            pltpu.VMEM((8, 2 * ROWS), F32),
            pltpu.VMEM((ROWS, KV), BF16),
            pltpu.VMEM((ROWS, KV), BF16),
            pltpu.VMEM((4, ROWS, BLK), BF16),
            pltpu.VMEM((4, 8, BLK), F32),
            pltpu.VMEM((4, 8, BLK), F32),
            pltpu.VMEM((4, 256, 1024), BF16),
            pltpu.VMEM((4, 256, 1024), BF16),
            pltpu.VMEM((256, 512), BF16),
            pltpu.VMEM((2, 128, 512), BF16),
            pltpu.VMEM((2, 256, 512), BF16),
            pltpu.VMEM((2, 256, 512), BF16),
            pltpu.VMEM((4, 256, 128), BF16),
            pltpu.VMEM((256, 128), F32),
            pltpu.VMEM((2, 128, 128), BF16),
            pltpu.VMEM((2, 256, 128), BF16),
            pltpu.VMEM((4, 256, 128), F32),
            pltpu.VMEM((4, 256, 128), F32),
            pltpu.VMEM((4, 256, 512), BF16),
            pltpu.VMEM((4, 256, 512), BF16),
            pltpu.SMEM((1,), jnp.int32),
            pltpu.SemaphoreType.DMA((N_REMOTE,)),
            pltpu.SemaphoreType.DMA((N_REMOTE,)),
            pltpu.SemaphoreType.DMA((N_LOCAL,)),
        ],
        compiler_params=pltpu.CompilerParams(
            collective_id=0, has_side_effects=True, vmem_limit_bytes=52 * 1024 * 1024
        ),
        cost_estimate=pl.CostEstimate(
            flops=6 * ROWS * D * KV, bytes_accessed=24 << 20, transcendentals=ROWS
        ),
    )(x, gain, w, cot, frag, params, moment, index)
    return pl.pallas_call(
        store,
        out_shape=(
            out((ROWS, KV), BF16), out((ROWS, D), BF16), out((1, BLK, KV), BF16),
            out((1, BLK), BF16), out((256, 128), F32), out((256, 128), F32),
            out((256, D), BF16),
        ),
        in_specs=[vmem] * 7,
        out_specs=(any_spec, any_spec, any_spec, vmem, any_spec, any_spec, any_spec),
        scratch_shapes=[pltpu.SemaphoreType.DMA((6,))],
        compiler_params=pltpu.CompilerParams(vmem_limit_bytes=2 * 1024 * 1024),
    )(*held)


def solution(mesh):
    return jax.shard_map(
        on_device,
        mesh=mesh,
        in_specs=(
            P(("rep", "fsdp"), None),
            P("rep", "fsdp"),
            P("rep", "fsdp", None),
            P(("rep", "fsdp"), None),
            P("rep", "fsdp", None),
            P(None, "fsdp", "rep"),
            P(None, "fsdp", "rep"),
            P(),
        ),
        out_specs=(
            P(("rep", "fsdp"), None),
            P(("rep", "fsdp"), None),
            P("rep", "fsdp", None),
            P("rep", "fsdp"),
            P("fsdp", "rep"),
            P("fsdp", "rep"),
            P("fsdp", None),
        ),
        check_vma=False,
    )
```

```python
import jax
import jax.numpy as jnp
from jax import lax
from jax.experimental import pallas as pl
from jax.experimental.pallas import tpu as pltpu
from jax.sharding import PartitionSpec as P

MESH = pl.DeviceIdType.MESH
F32, BF16 = jnp.float32, jnp.bfloat16
D = 4096
ROWS = 256
BLK = 512
KV = 1024
CH = 32

N_COT, N_X, N_W, N_GAIN, N_INV = 0, 1, 5, 9, 12
N_WF, N_KV1, N_Z2, N_ZG2 = 50, 52, 53, 55
N_COT1, N_S2B, N_S1PB, N_S1SB = 57, 58, 60, 62
N_S2, N_S1P, N_S1S, N_INNER, N_KV, N_DX, N_GG = 13, 15, 17, 19, 20, 21, 25
N_FR, N_Y1, N_Y2, N_Z1, N_ZG1, N_G1, N_G2, N_SY = 28, 32, 34, 36, 39, 42, 44, 46
N_REMOTE = 64
L_X, L_C, L_W, L_FR, L_OP, L_OM, L_IDX = 0, 8, 9, 10, 14, 15, 16
N_LOCAL = 17


def wide(value, times):
    return jnp.concatenate([value] * times, axis=1)


def kernel(
    x_hbm, gain_ref, w_hbm, c_hbm, fr_hbm, op_hbm, om_hbm, idx_hbm,
    kv_out, dx_out, dw_out, dg_out, np_out, nm_out, sy_out,
    xv, xp, cv, wv, gv, inv, nv, hv, kacc, d0, d13, s2, s2r, s1, s1r,
    inn, ins, inr, kvs, kvr, dxs, gs, gr,
    fo, fr, f2, y1r, f13, y2r, gb, g0, z1r, zr, opv, omv, sy, sp, idx_ref,
    ssem, rsem, lsem,
):
    f, r = lax.axis_index("fsdp"), lax.axis_index("rep")
    x, z = f // 2, f % 2
    y, zh, c = r // 8, (r // 2) % 4, r % 2

    def at_x(step):
        return {"fsdp": ((x + step) % 4) * 2 + z}

    def at_y(step):
        return {"rep": ((y + step) % 4) * 8 + zh * 2 + c}

    def at_zh(step):
        return {"rep": y * 8 + ((zh + step) % 4) * 2 + c}

    pair, core = {"fsdp": x * 2 + 1 - z}, {"rep": y * 8 + zh * 2 + 1 - c}

    def remote(number, source, target, device):
        return pltpu.make_async_remote_copy(
            src_ref=source, dst_ref=target, send_sem=ssem.at[number], recv_sem=rsem.at[number],
            device_id=device, device_id_type=MESH,
        )

    def local(number, source, target):
        return pltpu.make_async_copy(source, target, lsem.at[number])

    def own_cols(j):
        return pl.ds(pl.multiple_of((((x + j) % 4) * 2 + z) * BLK, BLK), BLK)

    def pair_cols(j):
        return pl.ds(pl.multiple_of((((x + j) % 4) * 2 + 1 - z) * BLK, BLK), BLK)

    def y_cols(k):
        return pl.ds(pl.multiple_of(((y + k) % 4) * 1024, 1024), 1024)

    low, high = pl.ds(0, ROWS), pl.ds(ROWS, ROWS)

    cols = (pl.ds(0, 512), pl.ds(512, 512))
    cot = [
        remote(number, c_hbm.at[:, cols[t]], cv.at[high, cols[t]], pair)
        for t, number in ((0, N_COT), (1, N_COT1))
    ]
    rows = [remote(N_X + j, x_hbm.at[:, pair_cols(j)], xp.at[j], pair) for j in range(4)]
    parts = (low, high)
    w_right = [remote(N_W + h, w_hbm.at[0, parts[h]], wv.at[3, parts[h]], at_x(1)) for h in range(2)]
    w_left = [remote(N_W + 2 + h, w_hbm.at[0, parts[h]], wv.at[1, parts[h]], at_x(3)) for h in range(2)]
    wf_right = remote(N_WF, wv.at[3, low], wv.at[2, low], at_x(1))
    wf_left = remote(N_WF + 1, wv.at[1, high], wv.at[2, high], at_x(3))
    gains = [remote(N_GAIN + m - 1, gv.at[0], gv.at[4 - m], at_x(m)) for m in (1, 2, 3)]
    inverse = remote(N_INV, inn.at[0], inn.at[1], pair)
    s2_right = [remote(n, s2.at[0, :, cols[t]], s2r.at[0, :, cols[t]], at_x(1)) for t, n in ((0, N_S2), (1, N_S2B))]
    s2_left = [remote(n + 1, s2.at[1, :, cols[t]], s2r.at[1, :, cols[t]], at_x(3)) for t, n in ((0, N_S2), (1, N_S2B))]
    s1p_right = [remote(n, s1.at[0, high, cols[t]], s1r.at[0, high, cols[t]], at_x(1)) for t, n in ((0, N_S1P), (1, N_S1PB))]
    s1p_left = [remote(n + 1, s1.at[1, low, cols[t]], s1r.at[1, low, cols[t]], at_x(3)) for t, n in ((0, N_S1P), (1, N_S1PB))]
    s1s_right = [remote(n, s1.at[0, low, cols[t]], s1r.at[0, low, cols[t]], at_x(1)) for t, n in ((0, N_S1S), (1, N_S1SB))]
    s1s_left = [remote(n + 1, s1.at[1, high, cols[t]], s1r.at[1, high, cols[t]], at_x(3)) for t, n in ((0, N_S1S), (1, N_S1SB))]
    inner = remote(N_INNER, ins, inr, pair)
    kv_half = [
        remote(number, kvs.at[pl.ds(p * 128, 128)], kvr.at[pl.ds(p * 128, 128)], pair)
        for p, number in ((0, N_KV), (1, N_KV1))
    ]
    dx_half = [remote(N_DX + j, dxs.at[j], dx_out.at[:, own_cols(j)], pair) for j in range(4)]
    gain_sum = [remote(N_GG + m - 1, gs.at[m], gr.at[m], at_x(m)) for m in (1, 2, 3)]
    frag = [remote(N_FR + k, fr_hbm.at[0, :, y_cols(k)], fr.at[k], core) for k in range(4)]
    y1_right = remote(N_Y1, f2.at[pl.ds(0, 128)], y1r.at[0], at_y(1))
    y1_left = remote(N_Y1 + 1, f2.at[pl.ds(128, 128)], y1r.at[1], at_y(3))
    y2_right = remote(N_Y2, f13.at[0], y2r.at[0], at_y(1))
    y2_left = remote(N_Y2 + 1, f13.at[1], y2r.at[1], at_y(3))
    top, bottom = pl.ds(0, 128), pl.ds(128, 128)
    z1_up = remote(N_Z1, gb.at[2, top], z1r.at[0], at_zh(1))
    z1_down = remote(N_Z1 + 1, gb.at[2, bottom], z1r.at[1], at_zh(3))
    z2_up = remote(N_Z2, gb.at[1], zr.at[0], at_zh(1))
    z2_down = remote(N_Z2 + 1, gb.at[3], zr.at[1], at_zh(3))

    def sy_cols(m):
        return pl.ds(pl.multiple_of(((zh + m) % 4) * 128, 128), 128)

    own_sy = sy.at[0, :, sy_cols(0)]
    zg1_up = remote(N_ZG1, own_sy, own_sy, at_zh(1))
    zg1_down = remote(N_ZG1 + 1, own_sy, own_sy, at_zh(3))
    below, above = sy.at[0, top, sy_cols(3)], sy.at[0, bottom, sy_cols(1)]
    zg2_up = remote(N_ZG2, below, below, at_zh(1))
    zg2_down = remote(N_ZG2 + 1, above, above, at_zh(3))
    g1_right = remote(N_G1, sy.at[0], sy.at[3], at_y(1))
    g1_left = remote(N_G1 + 1, sy.at[0], sy.at[1], at_y(3))
    g2_right = remote(N_G2, sy.at[3, top], sy.at[2, top], at_y(1))
    g2_left = remote(N_G2 + 1, sy.at[1, bottom], sy.at[2, bottom], at_y(3))
    to_core = [remote(N_SY + k, sy.at[k], sp.at[k], core) for k in range(4)]

    barrier = pltpu.get_barrier_semaphore()
    partners = [pair, core] + [at_x(m) for m in (1, 2, 3)]
    partners += [at_y(1), at_y(3)] + [at_zh(1), at_zh(3)]
    for device in partners:
        pl.semaphore_signal(barrier, inc=1, device_id=device, device_id_type=MESH)
    load_x = [local(L_X + j, x_hbm.at[:, own_cols(j)], xv.at[j]) for j in range(4)]
    load_x += [local(L_X + 4 + j, x_hbm.at[:, pair_cols(j)], xv.at[4 + j]) for j in range(4)]
    load_c = local(L_C, c_hbm, cv.at[low])
    load_w = local(L_W, w_hbm.at[0], wv.at[0])
    load_fr = [local(L_FR + k, fr_hbm.at[0, :, y_cols(k)], fo.at[k]) for k in range(4)]
    load_op, load_om = local(L_OP, op_hbm, opv), local(L_OM, om_hbm, omv)
    load_idx = local(L_IDX, idx_hbm, idx_ref)
    for copy in load_x + [load_idx, load_c, load_w] + load_fr + [load_op, load_om]:
        copy.start()

    gv[0] = jnp.broadcast_to(gain_ref[...].astype(F32), (8, BLK))
    pl.semaphore_wait(barrier, len(partners))

    w_right[0].start()
    rows[2].start()
    w_left[1].start()
    frag[2].start()
    cot[0].start()
    for copy in gains:
        copy.start()
    w_right[1].start()
    w_left[0].start()
    rows[1].start()
    for k in (1, 3, 0):
        frag[k].start()

    def chunks(count, body, carry=0, size=CH):
        def step(i, held):
            return body(pl.ds(pl.multiple_of(i * size, size), size), held)
        return lax.fori_loop(0, count // size, step, carry)

    def statistics(at, held):
        total = jnp.zeros((CH, BLK), F32)
        for j in range(8):
            value = xv[j, at, :].astype(F32)
            total = total + value * value
        mean = jnp.sum(total, axis=1, keepdims=True) * (1.0 / D)
        inv[0, at, :] = jnp.broadcast_to(lax.rsqrt(mean + 1e-05), (CH, 128))
        return held

    def normalise(j, half):
        source = xv if half == 0 else xp

        def step(at, held):
            unit = source[j, at, :].astype(F32) * wide(inv[half, at, :], BLK // 128)
            rows_at = pl.ds(pl.multiple_of(at.start + half * ROWS, CH), CH)
            nv[j, rows_at, :] = (unit * gv[j, 0:1, :]).astype(BF16)
            return held

        chunks(ROWS, step)

    def add_kv(j, first, at=pl.ds(0, 2 * ROWS)):
        def step(t, held):
            cols = pl.ds(pl.multiple_of(t * 256, 256), 256)
            part = jnp.dot(nv[j, at, :], wv[j, :, cols], preferred_element_type=F32)
            if first:
                kacc[at, cols] = part
            else:
                kacc[at, cols] += part
            return held

        lax.fori_loop(0, KV // 256, step, 0)

    def make_hidden(j):
        def step(t, held):
            at = pl.ds(pl.multiple_of(t * 256, 256), 256)
            hv[j, :, at] = lax.dot_general(
                cv[...], wv[j, at, :], (((1,), (1,)), ((), ())), preferred_element_type=F32
            )
            return held

        lax.fori_loop(0, BLK // 256, step, 0)

    def weight_term(j, half, t, put):
        put(cols[t], lax.dot_general(
            nv[j, :, pl.ds(half * 256, 256)], cv[:, cols[t]], (((0,), (0,)), ((), ())),
            preferred_element_type=F32,
        ))

    def into(ref, *where):
        def put(cols, value):
            ref[(*where, cols)] = value.astype(ref.dtype)
        return put

    def own_part(zz):
        return pl.ds(pl.multiple_of(zz * 256 + c * 128, 128), 128)

    def pair_sum(k, at, zz):
        cols = own_part(zz)
        return fo[k, at, cols].astype(F32) + fr[k, at, cols].astype(F32)

    for copy in load_x:
        copy.wait()
    chunks(ROWS, statistics)
    for half in range(2):
        part = pl.ds(half * 128, 128)
        inn[0, :, part] = jnp.transpose(inv[0, part, :])[0:8, :]
    inverse.start()

    for k in range(4):
        load_fr[k].wait()
    frag[2].wait_recv()

    def sum_f2(at, held):
        for zz in range(4):
            f2[at, pl.ds(zz * 128, 128)] = pair_sum(2, at, zz).astype(BF16)
        return held

    chunks(256, sum_f2)
    y1_right.start()
    y1_left.start()

    for copy in gains:
        copy.wait_recv()
    for j in (2, 1, 3, 0):
        normalise(j, 0)

    y1_right.wait_recv()
    y1_left.wait_recv()

    def sum_f13(side, k, half):
        def plain(at, held):
            there = pl.ds(pl.multiple_of(at.start + (1 - half) * 128, CH), CH)
            for zz in range(4):
                f13[side, there, pl.ds(zz * 128, 128)] = pair_sum(k, there, zz).astype(BF16)
            return held

        def passing(at, held):
            there = pl.ds(pl.multiple_of(at.start + half * 128, CH), CH)
            for zz in range(4):
                cols = pl.ds(zz * 128, 128)
                total = pair_sum(k, there, zz) + y1r[side, at, cols].astype(F32)
                f13[side, there, cols] = total.astype(BF16)
            return held

        frag[k].wait_recv()
        chunks(128, passing)
        chunks(128, plain)

    sum_f13(0, 1, 0)
    y2_right.start()
    sum_f13(1, 3, 1)
    y2_left.start()

    w_right[0].wait_recv()
    wf_right.start()
    w_left[1].wait_recv()
    wf_left.start()

    load_c.wait()
    load_w.wait()
    rows[2].wait_send()
    rows[3].start()

    frag[0].wait_recv()
    y2_right.wait_recv()
    y2_left.wait_recv()

    def sum_g(m):
        zz = (zh + m) % 4
        cols = pl.ds(pl.multiple_of(zz * 128, 128), 128)

        def step(at, held):
            total = pair_sum(0, at, zz)
            total = total + y2r[0, at, cols].astype(F32) + y2r[1, at, cols].astype(F32)
            if m == 0:
                g0[at, :] = total
            else:
                gb[m, at, :] = total.astype(BF16)
            return held

        chunks(256, step)

    sum_g(2)
    z1_up.start()
    z1_down.start()
    for m in (1, 3, 0):
        sum_g(m)

    inverse.wait_recv()
    for half in range(2):
        part = pl.ds(half * 128, 128)
        inv[1, part, :] = jnp.transpose(jnp.broadcast_to(inn[1, 0:1, part], (128, 128)))
    rows[2].wait_recv()
    rows[0].start()
    normalise(2, 1)
    cot[0].wait_recv()
    weight_term(2, 0, 0, into(s2, 0, slice(None)))
    s2_right[0].start()
    weight_term(2, 1, 0, into(s2, 1, slice(None)))
    s2_left[0].start()

    def pass_g(side, m, first_row):
        def step(at, held):
            there = pl.ds(pl.multiple_of(at.start + first_row, CH), CH)
            total = gb[m, there, :].astype(F32) + z1r[side, at, :].astype(F32)
            gb[m, there, :] = total.astype(BF16)
            return held

        chunks(128, step)

    z1_up.wait_recv()
    z1_down.wait_recv()
    pass_g(0, 1, 0)
    z2_up.start()
    pass_g(1, 3, 128)
    z2_down.start()

    rows[1].wait_recv()
    rows[1].wait_send()
    cot[1].start()
    normalise(1, 1)
    weight_term(1, 1, 0, into(s1, 0, high))
    s1p_right[0].start()
    weight_term(1, 0, 0, into(d13, 0, slice(None)))
    rows[3].wait_recv()
    normalise(3, 1)
    weight_term(3, 0, 0, into(s1, 1, low))
    s1p_left[0].start()
    weight_term(3, 1, 0, into(d13, 1, slice(None)))

    w_right[1].wait_recv()
    w_left[0].wait_recv()
    add_kv(1, True)
    add_kv(3, False)
    wf_right.wait_recv()
    wf_left.wait_recv()
    add_kv(2, False)
    add_kv(0, False, low)

    def inner_step(half):
        def step(at, held):
            there = pl.ds(pl.multiple_of(at.start + half * ROWS, CH), CH)
            product = jnp.zeros((CH, 256), F32)
            for t in range(4):
                cols = pl.ds(t * 256, 256)
                product = product + cv[there, cols].astype(F32) * kacc[there, cols]
            total = jnp.sum(product, axis=1, keepdims=True) * (1.0 / D)
            inv[2 + half, at, :] = jnp.broadcast_to(total, (CH, 128))
            return held

        chunks(ROWS, step)
        for part in range(2):
            there = pl.ds(half * ROWS + part * 128, 128)
            ins[:, there] = jnp.transpose(inv[2 + half, pl.ds(part * 128, 128), :])[0:8, :]

    def round_kv(part):
        def step(at, held):
            there = pl.ds(pl.multiple_of(at.start + part * 128, CH), CH)
            source = pl.ds(pl.multiple_of(at.start + part * 128 + ROWS, CH), CH)
            kvs[there, :] = kacc[source, :].astype(BF16)
            return held

        chunks(128, step)

    z2_up.wait_recv()
    z2_down.wait_recv()
    load_op.wait()
    load_om.wait()
    load_idx.wait()
    chosen = idx_ref[0]

    def update(at, held):
        total = g0[at, :] + zr[0, at, :].astype(F32) + zr[1, at, :].astype(F32)
        now = opv[chosen, at, :]
        pseudo = now - total * (1.0 / 32.0)
        moment = 0.9 * omv[chosen, at, :] + pseudo
        new = now - 0.7 * (pseudo + 0.9 * moment)
        nm_out[at, :] = moment
        np_out[at, :] = new
        sy[0, at, sy_cols(0)] = new.astype(BF16)
        return held

    chunks(256, update)

    inner_step(0)
    rows[0].wait_recv()
    zg1_up.start()
    zg1_down.start()
    normalise(0, 1)
    add_kv(0, False, high)
    round_kv(0)
    kv_half[0].start()
    round_kv(1)

    cot[1].wait_recv()
    inner_step(1)
    inner.start()
    kv_half[1].start()
    weight_term(2, 0, 1, into(s2, 0, slice(None)))
    s2_right[1].start()
    weight_term(2, 1, 1, into(s2, 1, slice(None)))
    s2_left[1].start()
    weight_term(1, 1, 1, into(s1, 0, high))
    s1p_right[1].start()
    weight_term(3, 0, 1, into(s1, 1, low))
    s1p_left[1].start()
    for j in range(4):
        make_hidden(j)

    def add_passing(side, first_row, t):
        def step(at, held):
            there = pl.ds(pl.multiple_of(at.start + first_row, CH), CH)
            total = d13[side, at, cols[t]] + s2r[side, at, cols[t]].astype(F32)
            s1[side, there, cols[t]] = total.astype(BF16)
            return held
        chunks(256, step)

    def pass_on(t):
        s2_right[t].wait_recv()
        add_passing(0, 0, t)
        s1s_right[t].start()
        s2_left[t].wait_recv()
        add_passing(1, 256, t)
        s1s_left[t].start()

    inner.wait_recv()
    for half in range(2):
        for part in range(2):
            mine = pl.ds(half * ROWS + part * 128, 128)
            theirs = pl.ds((1 - half) * ROWS + part * 128, 128)
            total = ins[0:1, mine] + inr[0:1, theirs]
            inv[2 + half, pl.ds(part * 128, 128), :] = jnp.transpose(
                jnp.broadcast_to(total, (128, 128))
            )

    def input_grad(j, half, put):
        source = xv if half == 0 else xp

        def step(at, held):
            there = pl.ds(pl.multiple_of(at.start + half * ROWS, CH), CH)
            scale = wide(inv[half, at, :], BLK // 128)
            unit = source[j, at, :].astype(F32) * scale
            hidden = hv[j, there, :]
            term = (hidden * unit).reshape(CH // 8, 8, BLK)
            scaled = hidden * gv[j, 0:1, :]
            mean = wide(inv[2 + half, at, :], BLK // 128)
            put(at, (scale * (scaled - unit * mean)).astype(BF16))
            return held + jnp.sum(term, axis=0)

        return chunks(ROWS, step, jnp.zeros((8, BLK), F32))

    def put_pair(j):
        def put(at, value):
            dxs[j, at, :] = value
        return put

    def put_own(j):
        def put(at, value):
            dx_out[at, own_cols(j)] = value
        return put

    for j in range(4):
        gs[j] = input_grad(j, 1, put_pair(j))
        dx_half[j].start()
        if j == 0:
            zg1_up.wait_recv()
            zg2_up.start()
            zg1_down.wait_recv()
            zg2_down.start()

    pass_on(0)
    weight_term(1, 0, 1, into(d13, 0, slice(None)))
    weight_term(3, 1, 1, into(d13, 1, slice(None)))
    pass_on(1)

    zg2_up.wait_recv()
    zg2_down.wait_recv()
    g1_right.start()
    g1_left.start()
    to_core[0].start()

    for j in (1, 2, 3, 0):
        total = gs[j] + input_grad(j, 0, put_own(j))
        gs[j] = jnp.broadcast_to(jnp.sum(total, axis=0, keepdims=True), (8, BLK))
        if j > 0:
            gain_sum[j - 1].start()

    g1_right.wait_recv()
    g2_right.start()
    g1_left.wait_recv()
    g2_left.start()
    to_core[3].start()
    to_core[1].start()

    for t in range(2):
        weight_term(0, 0, t, into(d0, low))
        weight_term(0, 1, t, into(d0, high))

    def place(k):
        to_core[k].wait_recv()
        first = ((y + k) % 4) * 1024

        def step(at, held):
            for zz in range(4):
                cols = pl.ds(zz * 128, 128)
                mine = pl.ds(pl.multiple_of(first + zz * 256 + c * 128, 128), 128)
                theirs = pl.ds(pl.multiple_of(first + zz * 256 + (1 - c) * 128, 128), 128)
                sy_out[at, mine] = sy[k, at, cols]
                sy_out[at, theirs] = sp[k, at, cols]
            return held

        chunks(256, step)

    place(0)
    g2_right.wait_recv()
    g2_left.wait_recv()
    to_core[2].start()
    place(3)
    place(1)

    for copy in kv_half:
        copy.wait_recv()

    def finish_kv(at, held):
        kv_out[at, :] = (kacc[at, :] + kvr[at, :].astype(F32)).astype(BF16)
        return held

    chunks(ROWS, finish_kv)
    place(2)
    for copy in gain_sum:
        copy.wait_recv()
    dg_out[...] = gs[0] + gr[1] + gr[2] + gr[3]
    for copy in s1p_right + s1p_left + s1s_right + s1s_left:
        copy.wait_recv()

    def finish_dw(at, held):
        total = d0[at, :] + s1r[0, at, :].astype(F32) + s1r[1, at, :].astype(F32)
        dw_out[at, :] = total.astype(BF16)
        return held

    chunks(BLK, finish_dw)
    for copy in dx_half:
        copy.wait_recv()

    for copy in (
        w_right + w_left + cot + [rows[3], rows[0], wf_right, wf_left, inverse, inner]
        + s2_right + s2_left + s1p_right + s1p_left + s1s_right + s1s_left
        + kv_half
        + [y1_right, y1_left, y2_right, y2_left, g1_right, g1_left, g2_right, g2_left]
        + gains + dx_half + gain_sum + frag + [zg1_up, zg1_down, zg2_up, zg2_down] + [z1_up, z1_down, z2_up, z2_down] + to_core
    ):
        copy.wait_send()


def store(kv, dx, dw, dg, np_, nm, sy, kv_out, dx_out, dw_out, dg_out, np_out, nm_out, sy_out, sem):
    copies = [
        pltpu.make_async_copy(source, target, sem.at[i])
        for i, (source, target) in enumerate(
            ((dx, dx_out), (sy, sy_out), (dw, dw_out.at[0]), (kv, kv_out), (np_, np_out), (nm, nm_out))
        )
    ]
    for copy in copies:
        copy.start()
    dg_out[...] = dg[0:1, :].astype(BF16)
    for copy in copies:
        copy.wait()


def on_device(x, gain, w, cot, frag, params, moment, index):
    any_spec = pl.BlockSpec(memory_space=pl.ANY)
    vmem = pl.BlockSpec(memory_space=pltpu.VMEM)
    out = jax.ShapeDtypeStruct
    held = pl.pallas_call(
        kernel,
        out_shape=(
            pltpu.VMEM((ROWS, KV), BF16), pltpu.VMEM((ROWS, D), BF16), pltpu.VMEM((BLK, KV), BF16),
            pltpu.VMEM((8, BLK), F32), pltpu.VMEM((256, 128), F32), pltpu.VMEM((256, 128), F32),
            pltpu.VMEM((256, D), BF16),
        ),
        in_specs=[any_spec, vmem] + [any_spec] * 6,
        out_specs=(vmem,) * 7,
        scratch_shapes=[
            pltpu.VMEM((8, ROWS, BLK), BF16),
            pltpu.VMEM((4, ROWS, BLK), BF16),
            pltpu.VMEM((2 * ROWS, KV), BF16),
            pltpu.VMEM((4, BLK, KV), BF16),
            pltpu.VMEM((4, 8, BLK), F32),
            pltpu.VMEM((4, ROWS, 128), F32),
            pltpu.VMEM((4, 2 * ROWS, BLK), BF16),
            pltpu.VMEM((4, 2 * ROWS, BLK), F32),
            pltpu.VMEM((2 * ROWS, KV), F32),
            pltpu.VMEM((BLK, KV), F32),
            pltpu.VMEM((2, 256, KV), F32),
            pltpu.VMEM((2, 256, KV), BF16),
            pltpu.VMEM((2, 256, KV), BF16),
            pltpu.VMEM((2, BLK, KV), BF16),
            pltpu.VMEM((2, BLK, KV), BF16),
            pltpu.VMEM((2, 8, ROWS), F32),
            pltpu.VMEM((8, 2 * ROWS), F32),
            pltpu.VMEM((8, 2 * ROWS), F32),
            pltpu.VMEM((ROWS, KV), BF16),
            pltpu.VMEM((ROWS, KV), BF16),
            pltpu.VMEM((4, ROWS, BLK), BF16),
            pltpu.VMEM((4, 8, BLK), F32),
            pltpu.VMEM((4, 8, BLK), F32),
            pltpu.VMEM((4, 256, 1024), BF16),
            pltpu.VMEM((4, 256, 1024), BF16),
            pltpu.VMEM((256, 512), BF16),
            pltpu.VMEM((2, 128, 512), BF16),
            pltpu.VMEM((2, 256, 512), BF16),
            pltpu.VMEM((2, 256, 512), BF16),
            pltpu.VMEM((4, 256, 128), BF16),
            pltpu.VMEM((256, 128), F32),
            pltpu.VMEM((2, 128, 128), BF16),
            pltpu.VMEM((2, 256, 128), BF16),
            pltpu.VMEM((4, 256, 128), F32),
            pltpu.VMEM((4, 256, 128), F32),
            pltpu.VMEM((4, 256, 512), BF16),
            pltpu.VMEM((4, 256, 512), BF16),
            pltpu.SMEM((1,), jnp.int32),
            pltpu.SemaphoreType.DMA((N_REMOTE,)),
            pltpu.SemaphoreType.DMA((N_REMOTE,)),
            pltpu.SemaphoreType.DMA((N_LOCAL,)),
        ],
        compiler_params=pltpu.CompilerParams(
            collective_id=0, has_side_effects=True, vmem_limit_bytes=52 * 1024 * 1024
        ),
        cost_estimate=pl.CostEstimate(
            flops=6 * ROWS * D * KV, bytes_accessed=24 << 20, transcendentals=ROWS
        ),
    )(x, gain, w, cot, frag, params, moment, index)
    return pl.pallas_call(
        store,
        out_shape=(
            out((ROWS, KV), BF16), out((ROWS, D), BF16), out((1, BLK, KV), BF16),
            out((1, BLK), BF16), out((256, 128), F32), out((256, 128), F32),
            out((256, D), BF16),
        ),
        in_specs=[vmem] * 7,
        out_specs=(any_spec, any_spec, any_spec, vmem, any_spec, any_spec, any_spec),
        scratch_shapes=[pltpu.SemaphoreType.DMA((6,))],
        compiler_params=pltpu.CompilerParams(vmem_limit_bytes=2 * 1024 * 1024),
    )(*held)


def solution(mesh):
    return jax.shard_map(
        on_device,
        mesh=mesh,
        in_specs=(
            P(("rep", "fsdp"), None),
            P("rep", "fsdp"),
            P("rep", "fsdp", None),
            P(("rep", "fsdp"), None),
            P("rep", "fsdp", None),
            P(None, "fsdp", "rep"),
            P(None, "fsdp", "rep"),
            P(),
        ),
        out_specs=(
            P(("rep", "fsdp"), None),
            P(("rep", "fsdp"), None),
            P("rep", "fsdp", None),
            P("rep", "fsdp"),
            P("fsdp", "rep"),
            P("fsdp", "rep"),
            P("fsdp", None),
        ),
        check_vma=False,
    )
```
